32 devices in a mesh: dp: 4 (over z), fsdp: 4 (over y, core), query: 2 (over x).
Axes of the slice: x: 2, y: 2, z: 4, core: 2. Of those that a mesh axis runs over, the one named last changes fastest.
Arguments:
- queries: bfloat16 [4, 1024, 1024], P('fsdp', ('dp', 'query')), may hold values from -40 to 40
- passages: bfloat16 [4, 2048, 1024], P('fsdp', ('dp', 'query')), may hold values from -6 to 6
- head_weight: bfloat16 [1024, 1024], P('fsdp'), may hold values from -0.1875 to 0.1875
- positives: int32 [4, 1024], P('fsdp', ('dp', 'query')), may hold values from 0 to 2047
- negative_ids: int32 [4, 8, 2], P('fsdp', ('dp', 'query')), may hold values from 0 to 15, as said below
- negative_count: int32 [4, 8], P('fsdp', ('dp', 'query')), may hold values from 1 to 2, as said below
Outputs:
- query_loss: float32 [4, 1024], P('fsdp', ('dp', 'query'))
The draws below stay inside these ranges and needn't reach their ends.
Inputs may be any that keep to these rules, and one draw needn't show every extreme that they name: `negative_ids`: the 2 entries of a query block are distinct passage blocks of its index shard; only the first negative_count of them are live. `negative_count`: in every aligned run of 8 query blocks one has exactly 2 live entries.
All inputs are finite; a program needn't handle non-finite values.
Results may differ from the reference program's by a relative error of at most 0.0048.
Values may be sent and summed in bfloat16 or wider, within the bound.
A program may use at most 64 MiB of HBM per device.

```python
import jax
import jax.numpy as jnp
from jax import lax

E = 1024
BLOCK = 128
COLUMNS = 4
QCOL = 1024
CROWS = 2048
NQB = 8
NBC = 16
MAXL = 2


def list_draw(key):
    key_order, key_count, key_full, key_pos = jax.random.split(jax.random.fold_in(key, 101), 4)
    raw_scores = jax.random.randint(key_order, (COLUMNS, NQB, NBC), 0, 1 << 20)
    distinct = raw_scores * NBC + lax.broadcasted_iota(jnp.int32, (COLUMNS, NQB, NBC), 2)
    ordering = jnp.argsort(distinct, axis=2, stable=True).astype(jnp.int32)
    list_ids = ordering[:, :, :MAXL]
    least = (MAXL + 2) // 3
    counts = jax.random.randint(key_count, (COLUMNS, NQB), least, MAXL + 1)
    group_len = 8
    picked = jax.random.randint(key_full, (COLUMNS, NQB // group_len), 0, group_len)
    position = lax.broadcasted_iota(jnp.int32, (COLUMNS, NQB), 1) % group_len
    counts = jnp.where(position == jnp.repeat(picked, group_len, axis=1), MAXL, counts)
    targets = jax.random.randint(key_pos, (COLUMNS, QCOL), 0, CROWS)
    return (list_ids, counts.astype(jnp.int32), targets.astype(jnp.int32))


def float_draw(key):
    list_ids, counts, targets = list_draw(key)
    key_pas = jax.random.fold_in(jax.random.fold_in(key, 202), 0)
    key_que = jax.random.fold_in(jax.random.fold_in(key, 202), 1)
    key_pick = jax.random.fold_in(jax.random.fold_in(key, 202), 3)
    key_sign = jax.random.fold_in(jax.random.fold_in(key, 202), 4)
    key_dir = jax.random.fold_in(jax.random.fold_in(key, 202), 5)
    key_lift = jax.random.fold_in(jax.random.fold_in(key, 202), 6)
    passage_vals = jax.random.truncated_normal(key_pas, -4.0, 4.0, (COLUMNS, CROWS, E), jnp.float32)
    noise_vals = jax.random.truncated_normal(key_que, -6.0, 6.0, (COLUMNS, QCOL, E), jnp.float32)
    shared_dir = (jax.random.randint(key_dir, (COLUMNS, E), 0, 2) * 2 - 1).astype(jnp.float32)
    passage_vals = passage_vals + 2.0 * shared_dir[:, None, :]
    lift = jax.random.uniform(key_lift, (COLUMNS, QCOL, 1), jnp.float32, 0.0, 3.0)
    matched = jax.vmap(lambda table, index: table[index])(passage_vals, targets)
    query_vals = 0.3 * matched + noise_vals + lift * shared_dir[:, None, :]
    column_ids = jnp.arange(COLUMNS, dtype=jnp.int32)
    level = jnp.array([120.0, 180.0, 240.0], jnp.float32)[column_ids % 3]
    chosen_block = jax.random.randint(key_pick, (COLUMNS,), 0, NQB)
    query_row = chosen_block * BLOCK
    source_row = targets[column_ids, query_row]
    target_row = list_ids[column_ids, chosen_block, 0] * BLOCK + 1
    signs = (jax.random.randint(key_sign, (COLUMNS, E), 0, 2) * 2 - 1).astype(jnp.float32)
    source_vals = 3.0 * signs
    strength = level / (9.0 * E ** 0.5)
    passage_vals = passage_vals.at[column_ids, source_row].set(source_vals)
    query_vals = query_vals.at[column_ids, query_row].set(strength[:, None] * source_vals)
    shrink = 1.0 - 2.0 / level
    passage_vals = passage_vals.at[column_ids, target_row].set(shrink[:, None] * source_vals)
    return (query_vals, passage_vals)


def draw_queries(key, part):
    return float_draw(key)[0].astype(jnp.bfloat16)


def draw_passages(key, part):
    return float_draw(key)[1].astype(jnp.bfloat16)


def draw_positives(key, part):
    return list_draw(key)[2]


def draw_negative_ids(key, part):
    return list_draw(key)[0]


def draw_negative_count(key, part):
    return list_draw(key)[1]


def steps_of(rng, extent, cuts, low, top_value):
    loudness, own = 1.0, jax.random.fold_in(rng, 6)
    for axis_at, shards_of in cuts:
        draws = jnp.exp(jax.random.uniform(jax.random.fold_in(own, axis_at), (shards_of,), jnp.float32, low / len(cuts), top_value / len(cuts)))
        loudness = loudness * jnp.repeat(draws, extent[axis_at] // shards_of).reshape([-1 if axis == axis_at else 1 for axis in range(len(extent))])
    return loudness


def centred(rng, extent, width, bound, cuts=(), kind=jnp.bfloat16):
    factor_of = steps_of(rng, extent, cuts, -0.22, 0.18) if cuts else 1.0
    values = jax.random.normal(rng, extent, jnp.float32) * width * factor_of
    return jnp.minimum(jnp.maximum(values, -bound), bound).astype(kind)


def setup_inputs(seed: int = 0) -> dict:
    splits = jax.random.split(jax.random.key(seed), 7)
    return {
        "queries": draw_queries(jax.random.fold_in(splits[6], 71), 0),
        "passages": draw_passages(jax.random.fold_in(splits[6], 71), 0),
        "head_weight": centred(splits[2], (E, E), E ** -0.5, 0.1875, ((0, 4),)),
        "positives": draw_positives(jax.random.fold_in(splits[6], 71), 0),
        "negative_ids": draw_negative_ids(jax.random.fold_in(splits[6], 71), 0),
        "negative_count": draw_negative_count(jax.random.fold_in(splits[6], 71), 0),
    }


masked_floor = -1.0e30


def column_loss(queries, passages, head_weight, positives, negative_ids, negative_count):
    query_proj = jnp.dot(queries, head_weight, preferred_element_type=jnp.float32).astype(jnp.bfloat16)
    passage_proj = jnp.dot(passages, head_weight, preferred_element_type=jnp.float32).astype(jnp.bfloat16)
    scale_factor = E ** -0.5
    row_index = jnp.arange(CROWS, dtype=jnp.int32)
    live_slot = jnp.arange(MAXL, dtype=jnp.int32)[None, :] < negative_count[:, None]
    block_index = jnp.arange(NBC, dtype=jnp.int32)
    block_used = jnp.any((negative_ids[:, :, None] == block_index[None, None, :]) & live_slot[:, :, None], axis=1)

    def one_block(members):
        query_block, used_here, targets = members
        logits = jnp.dot(query_block, passage_proj.T, preferred_element_type=jnp.float32) * scale_factor
        is_target = row_index[None, :] == targets[:, None]
        chosen = jnp.repeat(used_here, BLOCK)[None, :] | is_target
        running_max = jnp.max(jnp.where(chosen, logits, masked_floor), axis=1)
        running_sum = jnp.sum(jnp.where(chosen, jnp.exp(logits - running_max[:, None]), 0.0), axis=1)
        target_logit = jnp.sum(jnp.where(is_target, logits, 0.0), axis=1)
        return running_max + jnp.log(running_sum) - target_logit

    shaped = (query_proj.reshape(NQB, BLOCK, E), block_used, positives.reshape(NQB, BLOCK))
    return lax.map(one_block, shaped).reshape(-1)


def reference(queries, passages, head_weight, positives, negative_ids, negative_count):
    def per_column(members):
        return column_loss(members[0], members[1], head_weight, members[2], members[3], members[4])

    return lax.map(per_column, (queries, passages, positives, negative_ids, negative_count))
```

```python
import functools

import jax
import jax.numpy as jnp
from jax import lax
from jax.experimental import pallas as pl
from jax.experimental.pallas import tpu as pltpu
from jax.sharding import PartitionSpec as P

BLOCK = 128
CORES = 2
PIECES = 2
MASKED = -1e30
MESH = pl.DeviceIdType.MESH


def kernel(
    sizes, q_ref, p_ref, w_ref, pos_ref, ids_ref, count_ref, out_ref,
    q_all, p_all, p_proj, w_all, meta, stats_out, stats_in,
    local_sem, q_send, q_recv, p_send, p_recv, own_send, own_recv,
    wy_send, wy_recv, wc_send, wc_recv, meta_send, meta_recv, st_send, st_recv,
):
    n, shards, pairs, max_list = sizes
    towers = shards // CORES
    rows_w = w_ref.shape[0]
    rows_p = p_ref.shape[1]
    width = q_ref.shape[2]
    piece_q = BLOCK // PIECES
    piece_w = rows_w // PIECES
    scale = width ** -0.5
    z = lax.axis_index("dp")
    f = lax.axis_index("fsdp")
    x = lax.axis_index("query")
    core = lax.rem(f, CORES)
    mate = f + 1 - 2 * core

    def remote(src, dst, send, recv, where):
        return pltpu.make_async_remote_copy(
            src_ref=src, dst_ref=dst, send_sem=send, recv_sem=recv,
            device_id=where, device_id_type=MESH,
        )

    def shard_rows(shard, c):
        start = pl.multiple_of(shard * rows_w + c * piece_w, piece_w)
        return w_all.at[pl.ds(start, piece_w)]

    own_w = w_all.at[pl.ds(pl.multiple_of(f * rows_w, rows_w), rows_w)]
    own_p = p_all.at[pl.ds(pl.multiple_of(x * rows_p, rows_p), rows_p)]
    locals_ = [
        pltpu.make_async_copy(w_ref, own_w, local_sem.at[0]),
        pltpu.make_async_copy(p_ref.at[0], own_p, local_sem.at[1]),
        pltpu.make_async_copy(q_ref.at[0], q_all.at[z], local_sem.at[2]),
    ]
    for copy in locals_:
        copy.start()

    barrier = pltpu.get_barrier_semaphore()
    friends = [{"dp": lax.rem(z + o, n)} for o in range(1, n)]
    friends += [{"query": lax.rem(x + o, pairs)} for o in range(1, pairs)]
    friends += [{"fsdp": lax.rem(f + CORES * o, shards)} for o in range(1, towers)]
    friends += [{"fsdp": mate}]
    for friend in friends:
        pl.semaphore_signal(barrier, inc=1, device_id=friend, device_id_type=MESH)

    meta[z, 0:1, :] = pos_ref[...]
    live = count_ref[0, 0]
    for l in range(max_list):
        entry = jnp.where(l < live, ids_ref[0, 0, l], -1)
        meta[z, l + 1:l + 2, :] = jnp.full((1, BLOCK), entry, jnp.int32)
    pl.semaphore_wait(barrier, len(friends))

    def q_copy(way, step, h):
        block = z - step if way == 0 else z + step
        block = jnp.clip(block, 0, n - 1)
        view = q_all.at[block, pl.ds(h * piece_q, piece_q)]
        src = q_ref.at[0, pl.ds(h * piece_q, piece_q)] if step == 0 else view
        target = jnp.minimum(z + 1, n - 1) if way == 0 else jnp.maximum(z - 1, 0)
        return remote(src, view, q_send.at[way, step, h], q_recv.at[way, step, h], {"dp": target})

    def q_sends(way, step):
        if way == 0:
            return (z + 1 < n) & (z >= step)
        return (z >= 1) & (z + step < n)

    def q_wait(way, step, h):
        block = z - 1 - step if way == 0 else z + 1 + step
        block = jnp.clip(block, 0, n - 1)
        view = q_all.at[block, pl.ds(h * piece_q, piece_q)]
        pltpu.make_async_copy(view, view, q_recv.at[way, step, h]).wait()

    def q_receives(way, step):
        return z - 1 - step >= 0 if way == 0 else z + 1 + step < n

    for h in range(PIECES):
        for way in range(2):
            @pl.when(q_sends(way, 0))
            def _():
                q_copy(way, 0, h).start()

    sent = []
    for c in range(PIECES):
        for o in range(1, towers):
            copy = remote(
                w_ref.at[pl.ds(c * piece_w, piece_w)], shard_rows(f, c),
                wy_send.at[o - 1, c], wy_recv.at[o - 1, c],
                {"fsdp": lax.rem(f + CORES * o, shards)},
            )
            copy.start()
            sent.append(copy)
    for o in range(1, pairs):
        copy = remote(
            p_ref.at[0], own_p, p_send.at[o - 1], p_recv.at[o - 1],
            {"query": lax.rem(x + o, pairs)},
        )
        copy.start()
        sent.append(copy)
    own_copy = remote(w_ref, own_w, own_send, own_recv, {"fsdp": mate})
    own_copy.start()
    sent.append(own_copy)
    for o in range(1, n):
        copy = remote(
            meta.at[z], meta.at[z], meta_send.at[o - 1], meta_recv.at[o - 1],
            {"dp": lax.rem(z + o, n)},
        )
        copy.start()
        sent.append(copy)

    def pass_queries(step, h):
        for way in range(2):
            @pl.when(q_receives(way, step))
            def _():
                q_wait(way, step, h)

            @pl.when(q_sends(way, step + 1))
            def _():
                q_copy(way, step + 1, h).start()

    def pass_weights(c):
        for o in range(1, towers):
            shard = lax.rem(f + shards - CORES * o, shards)
            view = shard_rows(shard, c)
            pltpu.make_async_copy(view, view, wy_recv.at[o - 1, c]).wait()
            copy = remote(view, view, wc_send.at[o - 1, c], wc_recv.at[o - 1, c], {"fsdp": mate})
            copy.start()
            sent.append(copy)

    events = [(step * PIECES + h, 0, (step, h)) for step in range(n - 2) for h in range(PIECES)]
    events += [(2 * c + 1, 1, c) for c in range(PIECES)]
    for _, kind, what in sorted(events):
        if kind == 0:
            pass_queries(*what)
        else:
            pass_weights(what)

    for copy in locals_:
        copy.wait()
    other_w = w_all.at[pl.ds(pl.multiple_of(mate * rows_w, rows_w), rows_w)]
    pltpu.make_async_copy(other_w, other_w, own_recv).wait()
    for c in range(PIECES):
        for o in range(1, towers):
            view = shard_rows(lax.rem(mate + shards - CORES * o, shards), c)
            pltpu.make_async_copy(view, view, wc_recv.at[o - 1, c]).wait()

    def project(rows):
        return jnp.dot(rows, w_all[...], preferred_element_type=jnp.float32).astype(jnp.bfloat16)

    for o in range(pairs):
        holder = lax.rem(x + pairs - o, pairs)
        part = pl.ds(pl.multiple_of(holder * rows_p, rows_p), rows_p)
        if o:
            view = p_all.at[part]
            pltpu.make_async_copy(view, view, p_recv.at[o - 1]).wait()
        p_proj[part, :] = project(p_all[part, :])

    for o in range(1, n):
        view = meta.at[lax.rem(z + n - o, n)]
        pltpu.make_async_copy(view, view, meta_recv.at[o - 1]).wait()

    tiles = pairs * rows_p // BLOCK
    first_tile = z * tiles
    row_index = lax.broadcasted_iota(jnp.int32, (BLOCK, BLOCK), 0)

    def stats_copy(block):
        return remote(
            stats_out.at[block], stats_in.at[z], st_send.at[block], st_recv.at[z], {"dp": block}
        )

    def meet(t, carry):
        away = lax.div(t + 1, 2)
        way = lax.rem(t + 1, 2)
        place = jnp.where(way == 0, z - away, z + away)
        block = jnp.clip(place, 0, n - 1)

        @pl.when((place >= 0) & (place < n))
        def _():
            @pl.when(away == n - 1)
            def _():
                for h in range(PIECES):
                    view = q_all.at[block, pl.ds(h * piece_q, piece_q)]
                    pltpu.make_async_copy(view, view, q_recv.at[way, n - 2, h]).wait()

            q_proj = project(q_all[block])
            logits = lax.dot_general(
                p_proj[...], q_proj, (((1,), (1,)), ((), ())),
                preferred_element_type=jnp.float32,
            ) * scale
            info = meta[block]
            target = info[0:1, :]
            top = jnp.full((1, BLOCK), MASKED, jnp.float32)
            target_logit = jnp.zeros((1, BLOCK), jnp.float32)
            picks = []
            for k in range(tiles):
                tile = logits[k * BLOCK:(k + 1) * BLOCK, :]
                listed = info[1:2, :] == first_tile + k
                for l in range(1, max_list):
                    listed = listed | (info[l + 1:l + 2, :] == first_tile + k)
                is_target = row_index == target - (first_tile + k) * BLOCK
                chosen = listed | is_target
                picks.append((tile, chosen))
                top = jnp.maximum(
                    top, jnp.max(jnp.where(chosen, tile, MASKED), axis=0, keepdims=True)
                )
                target_logit += jnp.sum(jnp.where(is_target, tile, 0.0), axis=0, keepdims=True)
            total = jnp.zeros((1, BLOCK), jnp.float32)
            for tile, chosen in picks:
                total += jnp.sum(
                    jnp.where(chosen, jnp.exp(tile - top), 0.0), axis=0, keepdims=True
                )

            @pl.when(t == 0)
            def _():
                stats_in[z, 0:1, :] = top
                stats_in[z, 1:2, :] = total
                stats_in[z, 2:3, :] = target_logit

            @pl.when(t > 0)
            def _():
                stats_out[block, 0:1, :] = top
                stats_out[block, 1:2, :] = total
                stats_out[block, 2:3, :] = target_logit
                stats_copy(block).start()

        return carry

    lax.fori_loop(0, 2 * n - 1, meet, 0)

    for o in range(1, n):
        view = stats_in.at[lax.rem(z + o, n)]
        pltpu.make_async_copy(view, view, st_recv.at[lax.rem(z + o, n)]).wait()
    top = stats_in[0, 0:1, :]
    for i in range(1, n):
        top = jnp.maximum(top, stats_in[i, 0:1, :])
    total = jnp.zeros((1, BLOCK), jnp.float32)
    target_logit = jnp.zeros((1, BLOCK), jnp.float32)
    for i in range(n):
        total += stats_in[i, 1:2, :] * jnp.exp(stats_in[i, 0:1, :] - top)
        target_logit += stats_in[i, 2:3, :]
    out_ref[...] = top + jnp.log(total) - target_logit

    for copy in sent:
        copy.wait_send()
    for step in range(n - 1):
        for way in range(2):
            @pl.when(q_sends(way, step))
            def _():
                for h in range(PIECES):
                    q_copy(way, step, h).wait_send()
    for o in range(1, n):
        stats_copy(lax.rem(z + o, n)).wait_send()


def local(sizes, queries, passages, head_weight, positives, negative_ids, negative_count):
    n, shards, pairs, max_list = sizes
    towers = shards // CORES
    width = queries.shape[2]
    rows_p = passages.shape[1]
    meta_rows = -(-(max_list + 1) // 8) * 8
    hops = max(n - 1, 1)
    dma = pltpu.SemaphoreType.DMA
    far = max(towers - 1, 1)
    return pl.pallas_call(
        functools.partial(kernel, sizes),
        out_shape=jax.ShapeDtypeStruct((1, BLOCK), jnp.float32),
        in_specs=[
            pl.BlockSpec(memory_space=pl.ANY),
            pl.BlockSpec(memory_space=pl.ANY),
            pl.BlockSpec(memory_space=pl.ANY),
            pl.BlockSpec(memory_space=pltpu.VMEM),
            pl.BlockSpec(memory_space=pltpu.SMEM),
            pl.BlockSpec(memory_space=pltpu.SMEM),
        ],
        out_specs=pl.BlockSpec(memory_space=pltpu.VMEM),
        scratch_shapes=[
            pltpu.VMEM((n, BLOCK, width), jnp.bfloat16),
            pltpu.VMEM((pairs * rows_p, width), jnp.bfloat16),
            pltpu.VMEM((pairs * rows_p, width), jnp.bfloat16),
            pltpu.VMEM((shards * head_weight.shape[0], width), jnp.bfloat16),
            pltpu.VMEM((n, meta_rows, BLOCK), jnp.int32),
            pltpu.VMEM((n, 8, BLOCK), jnp.float32),
            pltpu.VMEM((n, 8, BLOCK), jnp.float32),
            dma((3,)),
            dma((2, hops, PIECES)), dma((2, hops, PIECES)),
            dma((max(pairs - 1, 1),)), dma((max(pairs - 1, 1),)),
            dma, dma,
            dma((far, PIECES)), dma((far, PIECES)),
            dma((far, PIECES)), dma((far, PIECES)),
            dma((hops,)), dma((hops,)),
            dma((n,)), dma((n,)),
        ],
        compiler_params=pltpu.CompilerParams(
            collective_id=0, has_side_effects=True, vmem_limit_bytes=40 * 1024 * 1024
        ),
        name="retriever_loss",
    )(queries, passages, head_weight, positives, negative_ids, negative_count)


def solution(mesh):
    in_specs = (
        P("fsdp", ("dp", "query"), None),
        P("fsdp", ("dp", "query"), None),
        P("fsdp", None),
        P("fsdp", ("dp", "query")),
        P("fsdp", ("dp", "query"), None),
        P("fsdp", ("dp", "query")),
    )
    out_specs = P("fsdp", ("dp", "query"))

    def whole(queries, passages, head_weight, positives, negative_ids, negative_count):
        sizes = (
            mesh.shape["dp"], mesh.shape["fsdp"], mesh.shape["query"], negative_ids.shape[2]
        )
        return jax.shard_map(
            functools.partial(local, sizes),
            mesh=mesh, in_specs=in_specs, out_specs=out_specs, check_vma=False,
        )(queries, passages, head_weight, positives, negative_ids, negative_count)

    return whole
```

```python
import functools

import jax
import jax.numpy as jnp
from jax import lax
from jax.experimental import pallas as pl
from jax.experimental.pallas import tpu as pltpu
from jax.sharding import PartitionSpec as P

BLOCK = 128
CORES = 2
PIECES = 2
MASKED = -1e30
MESH = pl.DeviceIdType.MESH


def kernel(
    sizes, q_ref, p_ref, w_ref, pos_ref, ids_ref, count_ref, out_ref,
    q_all, p_all, p_proj, w_all, meta, stats_out, stats_in, ids_own, count_own,
    local_sem, q_send, q_recv, p_send, p_recv, own_send, own_recv,
    wy_send, wy_recv, wc_send, wc_recv, meta_send, meta_recv, st_send, st_recv,
):
    n, shards, pairs, max_list = sizes
    towers = shards // CORES
    rows_w = w_ref.shape[0]
    rows_p = p_ref.shape[1]
    width = q_ref.shape[2]
    piece_q = BLOCK // PIECES
    piece_w = rows_w // PIECES
    scale = width ** -0.5
    z = lax.axis_index("dp")
    f = lax.axis_index("fsdp")
    x = lax.axis_index("query")
    core = lax.rem(f, CORES)
    mate = f + 1 - 2 * core

    def remote(src, dst, send, recv, where):
        return pltpu.make_async_remote_copy(
            src_ref=src, dst_ref=dst, send_sem=send, recv_sem=recv,
            device_id=where, device_id_type=MESH,
        )

    def shard_rows(shard, c):
        start = pl.multiple_of(shard * rows_w + c * piece_w, piece_w)
        return w_all.at[pl.ds(start, piece_w)]

    own_w = w_all.at[pl.ds(pl.multiple_of(f * rows_w, rows_w), rows_w)]
    own_p = p_all.at[pl.ds(pl.multiple_of(x * rows_p, rows_p), rows_p)]
    lists_ = [
        pltpu.make_async_copy(pos_ref, meta.at[z, pl.ds(0, 1)], local_sem.at[3]),
        pltpu.make_async_copy(ids_ref, ids_own, local_sem.at[4]),
        pltpu.make_async_copy(count_ref, count_own, local_sem.at[5]),
    ]
    for copy in lists_:
        copy.start()
    locals_ = [
        pltpu.make_async_copy(w_ref, own_w, local_sem.at[0]),
        pltpu.make_async_copy(p_ref.at[0], own_p, local_sem.at[1]),
        pltpu.make_async_copy(q_ref.at[0], q_all.at[z], local_sem.at[2]),
    ]
    for copy in locals_:
        copy.start()

    barrier = pltpu.get_barrier_semaphore()
    friends = [{"dp": lax.rem(z + o, n)} for o in range(1, n)]
    friends += [{"query": lax.rem(x + o, pairs)} for o in range(1, pairs)]
    friends += [{"fsdp": lax.rem(f + CORES * o, shards)} for o in range(1, towers)]
    friends += [{"fsdp": mate}]
    for friend in friends:
        pl.semaphore_signal(barrier, inc=1, device_id=friend, device_id_type=MESH)

    for copy in lists_:
        copy.wait()
    live = count_own[0, 0]
    for l in range(max_list):
        entry = jnp.where(l < live, ids_own[0, 0, l], -1)
        meta[z, l + 1:l + 2, :] = jnp.full((1, BLOCK), entry, jnp.int32)
    pl.semaphore_wait(barrier, len(friends))

    def q_copy(way, step, h):
        block = z - step if way == 0 else z + step
        block = jnp.clip(block, 0, n - 1)
        view = q_all.at[block, pl.ds(h * piece_q, piece_q)]
        src = q_ref.at[0, pl.ds(h * piece_q, piece_q)] if step == 0 else view
        target = jnp.minimum(z + 1, n - 1) if way == 0 else jnp.maximum(z - 1, 0)
        return remote(src, view, q_send.at[way, step, h], q_recv.at[way, step, h], {"dp": target})

    def q_sends(way, step):
        if way == 0:
            return (z + 1 < n) & (z >= step)
        return (z >= 1) & (z + step < n)

    def q_wait(way, step, h):
        block = z - 1 - step if way == 0 else z + 1 + step
        block = jnp.clip(block, 0, n - 1)
        view = q_all.at[block, pl.ds(h * piece_q, piece_q)]
        pltpu.make_async_copy(view, view, q_recv.at[way, step, h]).wait()

    def q_receives(way, step):
        return z - 1 - step >= 0 if way == 0 else z + 1 + step < n

    for h in range(PIECES):
        for way in range(2):
            @pl.when(q_sends(way, 0))
            def _():
                q_copy(way, 0, h).start()

    sent = []
    for c in range(PIECES):
        for o in range(1, towers):
            copy = remote(
                w_ref.at[pl.ds(c * piece_w, piece_w)], shard_rows(f, c),
                wy_send.at[o - 1, c], wy_recv.at[o - 1, c],
                {"fsdp": lax.rem(f + CORES * o, shards)},
            )
            copy.start()
            sent.append(copy)
    for o in range(1, pairs):
        copy = remote(
            p_ref.at[0], own_p, p_send.at[o - 1], p_recv.at[o - 1],
            {"query": lax.rem(x + o, pairs)},
        )
        copy.start()
        sent.append(copy)
    own_copy = remote(w_ref, own_w, own_send, own_recv, {"fsdp": mate})
    own_copy.start()
    sent.append(own_copy)
    for o in range(1, n):
        copy = remote(
            meta.at[z], meta.at[z], meta_send.at[o - 1], meta_recv.at[o - 1],
            {"dp": lax.rem(z + o, n)},
        )
        copy.start()
        sent.append(copy)

    def pass_queries(step, h):
        for way in range(2):
            @pl.when(q_receives(way, step))
            def _():
                q_wait(way, step, h)

            @pl.when(q_sends(way, step + 1))
            def _():
                q_copy(way, step + 1, h).start()

    def pass_weights(c):
        for o in range(1, towers):
            shard = lax.rem(f + shards - CORES * o, shards)
            view = shard_rows(shard, c)
            pltpu.make_async_copy(view, view, wy_recv.at[o - 1, c]).wait()
            copy = remote(view, view, wc_send.at[o - 1, c], wc_recv.at[o - 1, c], {"fsdp": mate})
            copy.start()
            sent.append(copy)

    events = [(step * PIECES + h, 0, (step, h)) for step in range(n - 2) for h in range(PIECES)]
    events += [(2 * c + 1, 1, c) for c in range(PIECES)]
    for _, kind, what in sorted(events):
        if kind == 0:
            pass_queries(*what)
        else:
            pass_weights(what)

    for copy in locals_:
        copy.wait()
    other_w = w_all.at[pl.ds(pl.multiple_of(mate * rows_w, rows_w), rows_w)]
    pltpu.make_async_copy(other_w, other_w, own_recv).wait()
    for c in range(PIECES):
        for o in range(1, towers):
            view = shard_rows(lax.rem(mate + shards - CORES * o, shards), c)
            pltpu.make_async_copy(view, view, wc_recv.at[o - 1, c]).wait()

    def project(rows):
        return jnp.dot(rows, w_all[...], preferred_element_type=jnp.float32).astype(jnp.bfloat16)

    for o in range(pairs):
        holder = lax.rem(x + pairs - o, pairs)
        part = pl.ds(pl.multiple_of(holder * rows_p, rows_p), rows_p)
        if o:
            view = p_all.at[part]
            pltpu.make_async_copy(view, view, p_recv.at[o - 1]).wait()
        p_proj[part, :] = project(p_all[part, :])

    for o in range(1, n):
        view = meta.at[lax.rem(z + n - o, n)]
        pltpu.make_async_copy(view, view, meta_recv.at[o - 1]).wait()

    tiles = pairs * rows_p // BLOCK
    first_tile = z * tiles
    row_index = lax.broadcasted_iota(jnp.int32, (BLOCK, BLOCK), 0)

    def stats_copy(block):
        return remote(
            stats_out.at[block], stats_in.at[z], st_send.at[block], st_recv.at[z], {"dp": block}
        )

    def meet(t, carry):
        away = lax.div(t + 1, 2)
        way = lax.rem(t + 1, 2)
        place = jnp.where(way == 0, z - away, z + away)
        block = jnp.clip(place, 0, n - 1)

        @pl.when((place >= 0) & (place < n))
        def _():
            @pl.when(away == n - 1)
            def _():
                for h in range(PIECES):
                    view = q_all.at[block, pl.ds(h * piece_q, piece_q)]
                    pltpu.make_async_copy(view, view, q_recv.at[way, n - 2, h]).wait()

            q_proj = project(q_all[block])
            logits = lax.dot_general(
                p_proj[...], q_proj, (((1,), (1,)), ((), ())),
                preferred_element_type=jnp.float32,
            ) * scale
            info = meta[block]
            target = info[0:1, :]
            top = jnp.full((1, BLOCK), MASKED, jnp.float32)
            target_logit = jnp.zeros((1, BLOCK), jnp.float32)
            picks = []
            for k in range(tiles):
                tile = logits[k * BLOCK:(k + 1) * BLOCK, :]
                listed = info[1:2, :] == first_tile + k
                for l in range(1, max_list):
                    listed = listed | (info[l + 1:l + 2, :] == first_tile + k)
                is_target = row_index == target - (first_tile + k) * BLOCK
                chosen = listed | is_target
                picks.append((tile, chosen))
                top = jnp.maximum(
                    top, jnp.max(jnp.where(chosen, tile, MASKED), axis=0, keepdims=True)
                )
                target_logit += jnp.sum(jnp.where(is_target, tile, 0.0), axis=0, keepdims=True)
            total = jnp.zeros((1, BLOCK), jnp.float32)
            for tile, chosen in picks:
                total += jnp.sum(
                    jnp.where(chosen, jnp.exp(tile - top), 0.0), axis=0, keepdims=True
                )

            @pl.when(t == 0)
            def _():
                stats_in[z, 0:1, :] = top
                stats_in[z, 1:2, :] = total
                stats_in[z, 2:3, :] = target_logit

            @pl.when(t > 0)
            def _():
                stats_out[block, 0:1, :] = top
                stats_out[block, 1:2, :] = total
                stats_out[block, 2:3, :] = target_logit
                stats_copy(block).start()

        return carry

    lax.fori_loop(0, 2 * n - 1, meet, 0)

    for o in range(1, n):
        view = stats_in.at[lax.rem(z + o, n)]
        pltpu.make_async_copy(view, view, st_recv.at[lax.rem(z + o, n)]).wait()
    top = stats_in[0, 0:1, :]
    for i in range(1, n):
        top = jnp.maximum(top, stats_in[i, 0:1, :])
    total = jnp.zeros((1, BLOCK), jnp.float32)
    target_logit = jnp.zeros((1, BLOCK), jnp.float32)
    for i in range(n):
        total += stats_in[i, 1:2, :] * jnp.exp(stats_in[i, 0:1, :] - top)
        target_logit += stats_in[i, 2:3, :]
    out_ref[...] = top + jnp.log(total) - target_logit

    for copy in sent:
        copy.wait_send()
    for step in range(n - 1):
        for way in range(2):
            @pl.when(q_sends(way, step))
            def _():
                for h in range(PIECES):
                    q_copy(way, step, h).wait_send()
    for o in range(1, n):
        stats_copy(lax.rem(z + o, n)).wait_send()


def local(sizes, queries, passages, head_weight, positives, negative_ids, negative_count):
    n, shards, pairs, max_list = sizes
    towers = shards // CORES
    width = queries.shape[2]
    rows_p = passages.shape[1]
    meta_rows = -(-(max_list + 1) // 8) * 8
    hops = max(n - 1, 1)
    dma = pltpu.SemaphoreType.DMA
    far = max(towers - 1, 1)
    return pl.pallas_call(
        functools.partial(kernel, sizes),
        out_shape=jax.ShapeDtypeStruct((1, BLOCK), jnp.float32),
        in_specs=[
            pl.BlockSpec(memory_space=pltpu.HBM),
        ] * 6,
        out_specs=pl.BlockSpec(memory_space=pltpu.VMEM),
        scratch_shapes=[
            pltpu.VMEM((n, BLOCK, width), jnp.bfloat16),
            pltpu.VMEM((pairs * rows_p, width), jnp.bfloat16),
            pltpu.VMEM((pairs * rows_p, width), jnp.bfloat16),
            pltpu.VMEM((shards * head_weight.shape[0], width), jnp.bfloat16),
            pltpu.VMEM((n, meta_rows, BLOCK), jnp.int32),
            pltpu.VMEM((n, 8, BLOCK), jnp.float32),
            pltpu.VMEM((n, 8, BLOCK), jnp.float32),
            pltpu.SMEM(negative_ids.shape, jnp.int32),
            pltpu.SMEM(negative_count.shape, jnp.int32),
            dma((6,)),
            dma((2, hops, PIECES)), dma((2, hops, PIECES)),
            dma((max(pairs - 1, 1),)), dma((max(pairs - 1, 1),)),
            dma, dma,
            dma((far, PIECES)), dma((far, PIECES)),
            dma((far, PIECES)), dma((far, PIECES)),
            dma((hops,)), dma((hops,)),
            dma((n,)), dma((n,)),
        ],
        compiler_params=pltpu.CompilerParams(
            collective_id=0, has_side_effects=True, vmem_limit_bytes=64 * 1024 * 1024
        ),
        name="retriever_loss",
    )(queries, passages, head_weight, positives, negative_ids, negative_count)


def solution(mesh):
    in_specs = (
        P("fsdp", ("dp", "query"), None),
        P("fsdp", ("dp", "query"), None),
        P("fsdp", None),
        P("fsdp", ("dp", "query")),
        P("fsdp", ("dp", "query"), None),
        P("fsdp", ("dp", "query")),
    )
    out_specs = P("fsdp", ("dp", "query"))

    def whole(queries, passages, head_weight, positives, negative_ids, negative_count):
        sizes = (
            mesh.shape["dp"], mesh.shape["fsdp"], mesh.shape["query"], negative_ids.shape[2]
        )
        return jax.shard_map(
            functools.partial(local, sizes),
            mesh=mesh, in_specs=in_specs, out_specs=out_specs, check_vma=False,
        )(queries, passages, head_weight, positives, negative_ids, negative_count)

    return whole
```

```python
import functools

import jax
import jax.numpy as jnp
from jax import lax
from jax.experimental import pallas as pl
from jax.experimental.pallas import tpu as pltpu
from jax.sharding import PartitionSpec as P

BLOCK = 128
CORES = 2
PIECES = 2
MASKED = -1e30
MESH = pl.DeviceIdType.MESH


def kernel(
    sizes, q_ref, p_ref, w_ref, pos_ref, ids_ref, count_ref, out_ref,
    q_all, p_all, p_proj, w_all, meta, stats_out, stats_in, ids_own, count_own,
    p_far, q_far, far_out,
    local_sem, q_send, q_recv, p_send, p_recv, own_send, own_recv,
    wy_send, wy_recv, wc_send, wc_recv, meta_send, meta_recv, st_send, st_recv,
    pf_send, pf_recv, qf_send, qf_recv, mf_send, mf_recv, ex_send, ex_recv,
):
    n, shards, pairs, max_list = sizes
    towers = shards // CORES
    rows_w = w_ref.shape[0]
    rows_p = p_ref.shape[1]
    width = q_ref.shape[2]
    piece_q = BLOCK // PIECES
    piece_w = rows_w // PIECES
    scale = width ** -0.5
    z = lax.axis_index("dp")
    f = lax.axis_index("fsdp")
    x = lax.axis_index("query")
    core = lax.rem(f, CORES)
    mate = f + 1 - 2 * core

    short = n == 4 and pairs == 2
    folded = (core == 1) if short else False
    outer = (z == 0) | (z == n - 1)
    far = lax.rem(z + 2, n)
    beside = z + 1 - 2 * lax.rem(z, 2)
    across = lax.rem(x + 1, pairs)
    slots = n + 2 if short else n

    def remote(src, dst, send, recv, where):
        return pltpu.make_async_remote_copy(
            src_ref=src, dst_ref=dst, send_sem=send, recv_sem=recv,
            device_id=where, device_id_type=MESH,
        )

    def shard_rows(shard, c):
        start = pl.multiple_of(shard * rows_w + c * piece_w, piece_w)
        return w_all.at[pl.ds(start, piece_w)]

    own_w = w_all.at[pl.ds(pl.multiple_of(f * rows_w, rows_w), rows_w)]
    own_p = p_all.at[pl.ds(pl.multiple_of(x * rows_p, rows_p), rows_p)]
    lists_ = [
        pltpu.make_async_copy(pos_ref, meta.at[z, pl.ds(0, 1)], local_sem.at[3]),
        pltpu.make_async_copy(ids_ref, ids_own, local_sem.at[4]),
        pltpu.make_async_copy(count_ref, count_own, local_sem.at[5]),
    ]
    for copy in lists_:
        copy.start()
    locals_ = [
        pltpu.make_async_copy(w_ref, own_w, local_sem.at[0]),
        pltpu.make_async_copy(p_ref.at[0], own_p, local_sem.at[1]),
        pltpu.make_async_copy(q_ref.at[0], q_all.at[z], local_sem.at[2]),
    ]
    for copy in locals_:
        copy.start()

    barrier = pltpu.get_barrier_semaphore()
    friends = [{"dp": lax.rem(z + o, n)} for o in range(1, n)]
    friends += [{"query": lax.rem(x + o, pairs)} for o in range(1, pairs)]
    friends += [{"fsdp": lax.rem(f + CORES * o, shards)} for o in range(1, towers)]
    friends += [{"fsdp": mate}]
    if short:
        friends += [{"dp": far, "query": across}]
    for i in range(slots):
        stats_in[i, 0:1, :] = jnp.full((1, BLOCK), MASKED, jnp.float32)
        stats_in[i, 1:3, :] = jnp.zeros((2, BLOCK), jnp.float32)
    for friend in friends:
        pl.semaphore_signal(barrier, inc=1, device_id=friend, device_id_type=MESH)

    for copy in lists_:
        copy.wait()
    live = count_own[0, 0]
    for l in range(max_list):
        entry = jnp.where(l < live, ids_own[0, 0, l], -1)
        meta[z, l + 1:l + 2, :] = jnp.full((1, BLOCK), entry, jnp.int32)
    pl.semaphore_wait(barrier, len(friends))

    def q_copy(way, step, h):
        block = z - step if way == 0 else z + step
        block = jnp.clip(block, 0, n - 1)
        view = q_all.at[block, pl.ds(h * piece_q, piece_q)]
        src = q_ref.at[0, pl.ds(h * piece_q, piece_q)] if step == 0 else view
        target = jnp.minimum(z + 1, n - 1) if way == 0 else jnp.maximum(z - 1, 0)
        return remote(src, view, q_send.at[way, step, h], q_recv.at[way, step, h], {"dp": target})

    def q_sends(way, step):
        there = (z + 1 < n) & (z >= step) if way == 0 else (z >= 1) & (z + step < n)
        return there & jnp.logical_not(folded) if short and step == n - 2 else there

    def q_wait(way, step, h):
        block = z - 1 - step if way == 0 else z + 1 + step
        block = jnp.clip(block, 0, n - 1)
        view = q_all.at[block, pl.ds(h * piece_q, piece_q)]
        pltpu.make_async_copy(view, view, q_recv.at[way, step, h]).wait()

    def q_receives(way, step):
        return z - 1 - step >= 0 if way == 0 else z + 1 + step < n

    def qf_copy(h):
        part = pl.ds(h * piece_q, piece_q)
        return remote(
            q_all.at[far, part], q_far.at[part], qf_send.at[h], qf_recv.at[h], {"query": across}
        )

    def pf_copy():
        return remote(p_ref.at[0], p_far, pf_send, pf_recv, {"dp": beside})

    def mf_copy():
        return remote(meta.at[z], meta.at[n], mf_send, mf_recv, {"dp": far, "query": across})

    def ex_copy(i):
        where = {"dp": far, "query": across} if i else {"dp": far}
        return remote(far_out.at[i], stats_in.at[n + i], ex_send.at[i], ex_recv.at[i], where)

    for h in range(PIECES):
        for way in range(2):
            @pl.when(q_sends(way, 0))
            def _():
                q_copy(way, 0, h).start()

    sent = []
    for c in range(PIECES):
        for o in range(1, towers):
            copy = remote(
                w_ref.at[pl.ds(c * piece_w, piece_w)], shard_rows(f, c),
                wy_send.at[o - 1, c], wy_recv.at[o - 1, c],
                {"fsdp": lax.rem(f + CORES * o, shards)},
            )
            copy.start()
            sent.append(copy)
    for o in range(1, pairs):
        copy = remote(
            p_ref.at[0], own_p, p_send.at[o - 1], p_recv.at[o - 1],
            {"query": lax.rem(x + o, pairs)},
        )
        copy.start()
        sent.append(copy)
    if short:
        @pl.when(folded & outer)
        def _():
            pf_copy().start()
            mf_copy().start()
    own_copy = remote(w_ref, own_w, own_send, own_recv, {"fsdp": mate})
    own_copy.start()
    sent.append(own_copy)
    for o in range(1, n):
        copy = remote(
            meta.at[z], meta.at[z], meta_send.at[o - 1], meta_recv.at[o - 1],
            {"dp": lax.rem(z + o, n)},
        )
        copy.start()
        sent.append(copy)

    def pass_queries(step, h):
        for way in range(2):
            @pl.when(q_receives(way, step))
            def _():
                q_wait(way, step, h)

            @pl.when(q_sends(way, step + 1))
            def _():
                q_copy(way, step + 1, h).start()

        if short and step == 1:
            @pl.when(folded & jnp.logical_not(outer))
            def _():
                qf_copy(h).start()

    def pass_weights(c):
        for o in range(1, towers):
            shard = lax.rem(f + shards - CORES * o, shards)
            view = shard_rows(shard, c)
            pltpu.make_async_copy(view, view, wy_recv.at[o - 1, c]).wait()
            copy = remote(view, view, wc_send.at[o - 1, c], wc_recv.at[o - 1, c], {"fsdp": mate})
            copy.start()
            sent.append(copy)

    events = [(step * PIECES + h, 0, (step, h)) for step in range(n - 2) for h in range(PIECES)]
    events += [(2 * c + 1, 1, c) for c in range(PIECES)]
    for _, kind, what in sorted(events):
        if kind == 0:
            pass_queries(*what)
        else:
            pass_weights(what)

    for copy in locals_:
        copy.wait()
    other_w = w_all.at[pl.ds(pl.multiple_of(mate * rows_w, rows_w), rows_w)]
    pltpu.make_async_copy(other_w, other_w, own_recv).wait()
    for c in range(PIECES):
        for o in range(1, towers):
            view = shard_rows(lax.rem(mate + shards - CORES * o, shards), c)
            pltpu.make_async_copy(view, view, wc_recv.at[o - 1, c]).wait()

    def project(rows):
        return jnp.dot(rows, w_all[...], preferred_element_type=jnp.float32).astype(jnp.bfloat16)

    for o in range(pairs):
        holder = lax.rem(x + pairs - o, pairs)
        part = pl.ds(pl.multiple_of(holder * rows_p, rows_p), rows_p)
        if o:
            view = p_all.at[part]
            pltpu.make_async_copy(view, view, p_recv.at[o - 1]).wait()
        p_proj[part, :] = project(p_all[part, :])

    for o in range(1, n):
        view = meta.at[lax.rem(z + n - o, n)]
        pltpu.make_async_copy(view, view, meta_recv.at[o - 1]).wait()

    tiles = pairs * rows_p // BLOCK
    first_tile = z * tiles
    row_index = lax.broadcasted_iota(jnp.int32, (BLOCK, BLOCK), 0)

    def stats_copy(block):
        return remote(
            stats_out.at[block], stats_in.at[z], st_send.at[block], st_recv.at[z], {"dp": block}
        )

    def block_stats(q_proj, held, info, tile_id):
        logits = lax.dot_general(
            held, q_proj, (((1,), (1,)), ((), ())), preferred_element_type=jnp.float32
        ) * scale
        target = info[0:1, :]
        top = jnp.full((1, BLOCK), MASKED, jnp.float32)
        target_logit = jnp.zeros((1, BLOCK), jnp.float32)
        picks = []
        for k in range(held.shape[0] // BLOCK):
            tile = logits[k * BLOCK:(k + 1) * BLOCK, :]
            listed = info[1:2, :] == tile_id + k
            for l in range(1, max_list):
                listed = listed | (info[l + 1:l + 2, :] == tile_id + k)
            is_target = row_index == target - (tile_id + k) * BLOCK
            chosen = listed | is_target
            picks.append((tile, chosen))
            top = jnp.maximum(
                top, jnp.max(jnp.where(chosen, tile, MASKED), axis=0, keepdims=True)
            )
            target_logit += jnp.sum(jnp.where(is_target, tile, 0.0), axis=0, keepdims=True)
        total = jnp.zeros((1, BLOCK), jnp.float32)
        for tile, chosen in picks:
            total += jnp.sum(jnp.where(chosen, jnp.exp(tile - top), 0.0), axis=0, keepdims=True)
        return top, total, target_logit

    def meet(t, carry):
        away = lax.div(t + 1, 2)
        way = lax.rem(t + 1, 2)
        place = jnp.where(way == 0, z - away, z + away)
        block = jnp.clip(place, 0, n - 1)

        meets = (place >= 0) & (place < n)
        if short:
            meets = meets & jnp.logical_not(folded & (away == n - 1))

        @pl.when(meets)
        def _():
            @pl.when(away == n - 1)
            def _():
                for h in range(PIECES):
                    view = q_all.at[block, pl.ds(h * piece_q, piece_q)]
                    pltpu.make_async_copy(view, view, q_recv.at[way, n - 2, h]).wait()

            top, total, target_logit = block_stats(
                project(q_all[block]), p_proj[...], meta[block], first_tile
            )

            @pl.when(t == 0)
            def _():
                stats_in[z, 0:1, :] = top
                stats_in[z, 1:2, :] = total
                stats_in[z, 2:3, :] = target_logit

            @pl.when(t > 0)
            def _():
                stats_out[block, 0:1, :] = top
                stats_out[block, 1:2, :] = total
                stats_out[block, 2:3, :] = target_logit
                stats_copy(block).start()

        return carry

    lax.fori_loop(0, 2 * n - 1, meet, 0)

    if short:
        @pl.when(folded & jnp.logical_not(outer))
        def _():
            pltpu.make_async_copy(p_far, p_far, pf_recv).wait()
            held = project(p_far[...])
            far_tile = beside * tiles + x * (rows_p // BLOCK)
            for i in range(2):
                if i == 1:
                    for h in range(PIECES):
                        view = q_far.at[pl.ds(h * piece_q, piece_q)]
                        pltpu.make_async_copy(view, view, qf_recv.at[h]).wait()
                    view = meta.at[n]
                    pltpu.make_async_copy(view, view, mf_recv).wait()
                rows = q_far[...] if i else q_all[far]
                info = meta[n] if i else meta[far]
                found = block_stats(project(rows), held, info, far_tile)
                for j in range(3):
                    far_out[i, j:j + 1, :] = found[j]
                ex_copy(i).start()

    def reaches(other):
        ends = (z + other == n - 1) & outer
        return jnp.logical_not(folded & ends) if short else other >= 0

    for o in range(1, n):
        other = lax.rem(z + o, n)

        @pl.when(reaches(other))
        def _():
            view = stats_in.at[other]
            pltpu.make_async_copy(view, view, st_recv.at[other]).wait()

    if short:
        @pl.when(folded & outer)
        def _():
            for i in range(2):
                view = stats_in.at[n + i]
                pltpu.make_async_copy(view, view, ex_recv.at[i]).wait()
    top = stats_in[0, 0:1, :]
    for i in range(1, slots):
        top = jnp.maximum(top, stats_in[i, 0:1, :])
    total = jnp.zeros((1, BLOCK), jnp.float32)
    target_logit = jnp.zeros((1, BLOCK), jnp.float32)
    for i in range(slots):
        total += stats_in[i, 1:2, :] * jnp.exp(stats_in[i, 0:1, :] - top)
        target_logit += stats_in[i, 2:3, :]
    out_ref[...] = top + jnp.log(total) - target_logit

    for copy in sent:
        copy.wait_send()
    for step in range(n - 1):
        for way in range(2):
            @pl.when(q_sends(way, step))
            def _():
                for h in range(PIECES):
                    q_copy(way, step, h).wait_send()
    for o in range(1, n):
        other = lax.rem(z + o, n)

        @pl.when(reaches(other))
        def _():
            stats_copy(other).wait_send()
    if short:
        @pl.when(folded & outer)
        def _():
            pf_copy().wait_send()
            mf_copy().wait_send()

        @pl.when(folded & jnp.logical_not(outer))
        def _():
            for h in range(PIECES):
                qf_copy(h).wait_send()
            for i in range(2):
                ex_copy(i).wait_send()


def local(sizes, queries, passages, head_weight, positives, negative_ids, negative_count):
    n, shards, pairs, max_list = sizes
    towers = shards // CORES
    width = queries.shape[2]
    rows_p = passages.shape[1]
    meta_rows = -(-(max_list + 1) // 8) * 8
    hops = max(n - 1, 1)
    dma = pltpu.SemaphoreType.DMA
    far = max(towers - 1, 1)
    return pl.pallas_call(
        functools.partial(kernel, sizes),
        out_shape=jax.ShapeDtypeStruct((1, BLOCK), jnp.float32),
        in_specs=[
            pl.BlockSpec(memory_space=pltpu.HBM),
        ] * 6,
        out_specs=pl.BlockSpec(memory_space=pltpu.VMEM),
        scratch_shapes=[
            pltpu.VMEM((n, BLOCK, width), jnp.bfloat16),
            pltpu.VMEM((pairs * rows_p, width), jnp.bfloat16),
            pltpu.VMEM((pairs * rows_p, width), jnp.bfloat16),
            pltpu.VMEM((shards * head_weight.shape[0], width), jnp.bfloat16),
            pltpu.VMEM((n + 1, meta_rows, BLOCK), jnp.int32),
            pltpu.VMEM((n, 8, BLOCK), jnp.float32),
            pltpu.VMEM((n + 2, 8, BLOCK), jnp.float32),
            pltpu.SMEM(negative_ids.shape, jnp.int32),
            pltpu.SMEM(negative_count.shape, jnp.int32),
            pltpu.VMEM((rows_p, width), jnp.bfloat16),
            pltpu.VMEM((BLOCK, width), jnp.bfloat16),
            pltpu.VMEM((2, 8, BLOCK), jnp.float32),
            dma((6,)),
            dma((2, hops, PIECES)), dma((2, hops, PIECES)),
            dma((max(pairs - 1, 1),)), dma((max(pairs - 1, 1),)),
            dma, dma,
            dma((far, PIECES)), dma((far, PIECES)),
            dma((far, PIECES)), dma((far, PIECES)),
            dma((hops,)), dma((hops,)),
            dma((n,)), dma((n,)),
            dma, dma, dma((PIECES,)), dma((PIECES,)), dma, dma, dma((2,)), dma((2,)),
        ],
        compiler_params=pltpu.CompilerParams(
            collective_id=0, has_side_effects=True, vmem_limit_bytes=64 * 1024 * 1024
        ),
        name="retriever_loss",
    )(queries, passages, head_weight, positives, negative_ids, negative_count)


def solution(mesh):
    in_specs = (
        P("fsdp", ("dp", "query"), None),
        P("fsdp", ("dp", "query"), None),
        P("fsdp", None),
        P("fsdp", ("dp", "query")),
        P("fsdp", ("dp", "query"), None),
        P("fsdp", ("dp", "query")),
    )
    out_specs = P("fsdp", ("dp", "query"))

    def whole(queries, passages, head_weight, positives, negative_ids, negative_count):
        sizes = (
            mesh.shape["dp"], mesh.shape["fsdp"], mesh.shape["query"], negative_ids.shape[2]
        )
        return jax.shard_map(
            functools.partial(local, sizes),
            mesh=mesh, in_specs=in_specs, out_specs=out_specs, check_vma=False,
        )(queries, passages, head_weight, positives, negative_ids, negative_count)

    return whole
```

```python
import functools

import jax
import jax.numpy as jnp
from jax import lax
from jax.experimental import pallas as pl
from jax.experimental.pallas import tpu as pltpu
from jax.sharding import PartitionSpec as P

BLOCK = 128
CORES = 2
PIECES = 2
MASKED = -1e30
MESH = pl.DeviceIdType.MESH


def kernel(
    sizes, q_ref, p_ref, w_ref, pos_ref, ids_ref, count_ref, out_ref,
    q_all, p_all, p_proj, w_all, meta, stats_out, stats_in, ids_own, count_own,
    p_part, q_part, q_proj,
    local_sem, q_send, q_recv, p_send, p_recv, own_send, own_recv,
    wy_send, wy_recv, wc_send, wc_recv, meta_send, meta_recv, st_send, st_recv,
):
    n, shards, pairs, max_list = sizes
    towers = shards // CORES
    rows_w = w_ref.shape[0]
    rows_p = p_ref.shape[1]
    width = q_ref.shape[2]
    piece_q = BLOCK // PIECES
    piece_w = rows_w // PIECES
    piece_p = rows_p // PIECES
    scale = width ** -0.5
    z = lax.axis_index("dp")
    f = lax.axis_index("fsdp")
    x = lax.axis_index("query")
    core = lax.rem(f, CORES)
    mate = f + 1 - 2 * core

    def remote(src, dst, send, recv, where):
        return pltpu.make_async_remote_copy(
            src_ref=src, dst_ref=dst, send_sem=send, recv_sem=recv,
            device_id=where, device_id_type=MESH,
        )

    def shard_rows(shard, c):
        start = pl.multiple_of(shard * rows_w + c * piece_w, piece_w)
        return w_all.at[pl.ds(start, piece_w)]

    def p_rows(holder, h):
        return p_all.at[p_piece(holder, h)]

    def p_piece(holder, h):
        return pl.ds(pl.multiple_of(holder * rows_p + h * piece_p, piece_p), piece_p)

    own_w = w_all.at[pl.ds(pl.multiple_of(f * rows_w, rows_w), rows_w)]
    own_p = p_all.at[pl.ds(pl.multiple_of(x * rows_p, rows_p), rows_p)]
    lists_ = [
        pltpu.make_async_copy(pos_ref, meta.at[z, pl.ds(0, 1)], local_sem.at[3]),
        pltpu.make_async_copy(ids_ref, ids_own, local_sem.at[4]),
        pltpu.make_async_copy(count_ref, count_own, local_sem.at[5]),
    ]
    for copy in lists_:
        copy.start()
    locals_ = [
        pltpu.make_async_copy(w_ref, own_w, local_sem.at[0]),
        pltpu.make_async_copy(p_ref.at[0], own_p, local_sem.at[1]),
        pltpu.make_async_copy(q_ref.at[0], q_all.at[z], local_sem.at[2]),
    ]
    for copy in locals_:
        copy.start()

    barrier = pltpu.get_barrier_semaphore()
    friends = [{"dp": lax.rem(z + o, n)} for o in range(1, n)]
    friends += [{"query": lax.rem(x + o, pairs)} for o in range(1, pairs)]
    friends += [{"fsdp": lax.rem(f + CORES * o, shards)} for o in range(1, towers)]
    friends += [{"fsdp": mate}]
    for friend in friends:
        pl.semaphore_signal(barrier, inc=1, device_id=friend, device_id_type=MESH)

    for copy in lists_:
        copy.wait()
    live = count_own[0, 0]
    for l in range(max_list):
        entry = jnp.where(l < live, ids_own[0, 0, l], -1)
        meta[z, l + 1:l + 2, :] = jnp.full((1, BLOCK), entry, jnp.int32)
    pl.semaphore_wait(barrier, len(friends))

    def q_copy(way, step, h):
        block = z - step if way == 0 else z + step
        block = jnp.clip(block, 0, n - 1)
        view = q_all.at[block, pl.ds(h * piece_q, piece_q)]
        src = q_ref.at[0, pl.ds(h * piece_q, piece_q)] if step == 0 else view
        target = jnp.minimum(z + 1, n - 1) if way == 0 else jnp.maximum(z - 1, 0)
        return remote(src, view, q_send.at[way, step, h], q_recv.at[way, step, h], {"dp": target})

    def q_sends(way, step):
        if way == 0:
            return (z + 1 < n) & (z >= step)
        return (z >= 1) & (z + step < n)

    def q_wait(way, step, h):
        block = z - 1 - step if way == 0 else z + 1 + step
        block = jnp.clip(block, 0, n - 1)
        view = q_all.at[block, pl.ds(h * piece_q, piece_q)]
        pltpu.make_async_copy(view, view, q_recv.at[way, step, h]).wait()

    def q_receives(way, step):
        return z - 1 - step >= 0 if way == 0 else z + 1 + step < n

    for h in range(PIECES):
        for way in range(2):
            @pl.when(q_sends(way, 0))
            def _():
                q_copy(way, 0, h).start()

    sent = []
    for c in range(PIECES):
        for o in range(1, towers):
            copy = remote(
                w_ref.at[pl.ds(c * piece_w, piece_w)], shard_rows(f, c),
                wy_send.at[o - 1, c], wy_recv.at[o - 1, c],
                {"fsdp": lax.rem(f + CORES * o, shards)},
            )
            copy.start()
            sent.append(copy)
    for h in range(PIECES):
        for o in range(1, pairs):
            copy = remote(
                p_ref.at[0, pl.ds(h * piece_p, piece_p)], p_rows(x, h),
                p_send.at[o - 1, h], p_recv.at[o - 1, h], {"query": lax.rem(x + o, pairs)},
            )
            copy.start()
            sent.append(copy)
    own_copy = remote(w_ref, own_w, own_send, own_recv, {"fsdp": mate})
    own_copy.start()
    sent.append(own_copy)
    for o in range(1, n):
        copy = remote(
            meta.at[z], meta.at[z], meta_send.at[o - 1], meta_recv.at[o - 1],
            {"dp": lax.rem(z + o, n)},
        )
        copy.start()
        sent.append(copy)

    def pass_queries(step, h):
        for way in range(2):
            @pl.when(q_receives(way, step))
            def _():
                q_wait(way, step, h)

            @pl.when(q_sends(way, step + 1))
            def _():
                q_copy(way, step + 1, h).start()

    def pass_weights(c):
        for o in range(1, towers):
            shard = lax.rem(f + shards - CORES * o, shards)
            view = shard_rows(shard, c)
            pltpu.make_async_copy(view, view, wy_recv.at[o - 1, c]).wait()
            copy = remote(view, view, wc_send.at[o - 1, c], wc_recv.at[o - 1, c], {"fsdp": mate})
            copy.start()
            sent.append(copy)

    def span(shard, c, depth):
        return pl.ds(pl.multiple_of(shard * rows_w + c * piece_w, depth), depth)

    fine = piece_w % 128 == 0
    towers_from = [lax.rem(f - core + CORES * o, shards) for o in range(1, towers)]
    first_spans = [span(f - core, 0, CORES * rows_w)]
    if fine:
        piece_spans = [
            [span(base + k, c, piece_w) for base in towers_from for k in range(CORES)]
            for c in range(PIECES)
        ]
        last_spans = [one for c in range(1, PIECES) for one in piece_spans[c]]
    else:
        last_spans = [span(base, 0, CORES * rows_w) for base in towers_from]

    def partly(rows, spans):
        lhs = [rows[:, one] for one in spans]
        rhs = [w_all[one, :] for one in spans]
        lhs = lhs[0] if len(lhs) == 1 else jnp.concatenate(lhs, axis=1)
        rhs = rhs[0] if len(rhs) == 1 else jnp.concatenate(rhs, axis=0)
        return jnp.dot(lhs, rhs, preferred_element_type=jnp.float32)

    def project(rows):
        return jnp.dot(rows, w_all[...], preferred_element_type=jnp.float32).astype(jnp.bfloat16)

    def mate_weights(c):
        for o in range(1, towers):
            view = shard_rows(lax.rem(mate + shards - CORES * o, shards), c)
            pltpu.make_async_copy(view, view, wc_recv.at[o - 1, c]).wait()

    def neighbours(act):
        for way in range(2):
            @pl.when(q_receives(way, 0))
            def _():
                act(q_all.at[z - 1 if way == 0 else z + 1], q_part.at[1 + way])

    def begin(rows, part):
        part[...] = partly(rows, first_spans)

    def extend(rows, part):
        part[...] += partly(rows, piece_spans[0])

    own_part = p_part.at[pl.ds(pl.multiple_of(x * rows_p, rows_p), rows_p)]
    for copy in locals_:
        copy.wait()
    other_w = w_all.at[pl.ds(pl.multiple_of(mate * rows_w, rows_w), rows_w)]
    pltpu.make_async_copy(other_w, other_w, own_recv).wait()
    begin(own_p, own_part)
    begin(q_all.at[z], q_part.at[0])
    pass_queries(0, 0)
    pass_weights(0)
    pass_queries(0, 1)
    neighbours(begin)
    mate_weights(0)
    if fine:
        extend(own_p, own_part)
        extend(q_all.at[z], q_part.at[0])
        neighbours(extend)
    for o in range(1, pairs):
        holder = lax.rem(x + pairs - o, pairs)
        view = p_rows(holder, 0)
        pltpu.make_async_copy(view, view, p_recv.at[o - 1, 0]).wait()
        p_part[p_piece(holder, 0), :] = partly(
            view, first_spans + piece_spans[0] if fine else first_spans
        )
    for step in range(1, n - 2):
        pass_queries(step, 0)
        if step == 1:
            pass_weights(1)
        pass_queries(step, 1)
    mate_weights(1)

    for o in range(pairs):
        holder = lax.rem(x + pairs - o, pairs)
        for h in range(PIECES):
            view = p_rows(holder, h)
            piece = p_piece(holder, h)
            if o and h:
                pltpu.make_async_copy(view, view, p_recv.at[o - 1, h]).wait()
                p_proj[piece, :] = project(view[...])
            else:
                whole = p_part[piece, :] + partly(view, last_spans)
                p_proj[piece, :] = whole.astype(jnp.bfloat16)

    for o in range(1, n):
        view = meta.at[lax.rem(z + n - o, n)]
        pltpu.make_async_copy(view, view, meta_recv.at[o - 1]).wait()

    tiles = pairs * rows_p // BLOCK
    first_tile = z * tiles
    row_index = lax.broadcasted_iota(jnp.int32, (BLOCK, BLOCK), 0)

    def stats_copy(block):
        return remote(
            stats_out.at[block], stats_in.at[z], st_send.at[block], st_recv.at[z], {"dp": block}
        )

    def meet(t, carry):
        away = lax.div(t + 1, 2)
        way = lax.rem(t + 1, 2)
        place = jnp.where(way == 0, z - away, z + away)
        block = jnp.clip(place, 0, n - 1)

        @pl.when((place >= 0) & (place < n))
        def _():
            @pl.when(away <= 1)
            def _():
                rest = partly(q_all.at[block], last_spans)
                q_proj[...] = (q_part[jnp.minimum(t, 2)] + rest).astype(jnp.bfloat16)

            @pl.when((away > 1) & (away < n - 1))
            def _():
                q_proj[...] = project(q_all[block])

            @pl.when(away == n - 1)
            def _():
                for h in range(PIECES):
                    part = pl.ds(h * piece_q, piece_q)
                    view = q_all.at[block, part]
                    pltpu.make_async_copy(view, view, q_recv.at[way, n - 2, h]).wait()
                    q_proj[part, :] = project(view[...])

            logits = lax.dot_general(
                p_proj[...], q_proj[...], (((1,), (1,)), ((), ())),
                preferred_element_type=jnp.float32,
            ) * scale
            info = meta[block]
            target = info[0:1, :]
            top = jnp.full((1, BLOCK), MASKED, jnp.float32)
            target_logit = jnp.zeros((1, BLOCK), jnp.float32)
            picks = []
            for k in range(tiles):
                tile = logits[k * BLOCK:(k + 1) * BLOCK, :]
                listed = info[1:2, :] == first_tile + k
                for l in range(1, max_list):
                    listed = listed | (info[l + 1:l + 2, :] == first_tile + k)
                is_target = row_index == target - (first_tile + k) * BLOCK
                chosen = listed | is_target
                picks.append((tile, chosen))
                top = jnp.maximum(
                    top, jnp.max(jnp.where(chosen, tile, MASKED), axis=0, keepdims=True)
                )
                target_logit += jnp.sum(jnp.where(is_target, tile, 0.0), axis=0, keepdims=True)
            total = jnp.zeros((1, BLOCK), jnp.float32)
            for tile, chosen in picks:
                total += jnp.sum(
                    jnp.where(chosen, jnp.exp(tile - top), 0.0), axis=0, keepdims=True
                )

            @pl.when(t == 0)
            def _():
                stats_in[z, 0:1, :] = top
                stats_in[z, 1:2, :] = total
                stats_in[z, 2:3, :] = target_logit

            @pl.when(t > 0)
            def _():
                stats_out[block, 0:1, :] = top
                stats_out[block, 1:2, :] = total
                stats_out[block, 2:3, :] = target_logit
                stats_copy(block).start()

        return carry

    lax.fori_loop(0, 2 * n - 1, meet, 0)

    for o in range(1, n):
        view = stats_in.at[lax.rem(z + o, n)]
        pltpu.make_async_copy(view, view, st_recv.at[lax.rem(z + o, n)]).wait()
    top = stats_in[0, 0:1, :]
    for i in range(1, n):
        top = jnp.maximum(top, stats_in[i, 0:1, :])
    total = jnp.zeros((1, BLOCK), jnp.float32)
    target_logit = jnp.zeros((1, BLOCK), jnp.float32)
    for i in range(n):
        total += stats_in[i, 1:2, :] * jnp.exp(stats_in[i, 0:1, :] - top)
        target_logit += stats_in[i, 2:3, :]
    out_ref[...] = top + jnp.log(total) - target_logit

    for copy in sent:
        copy.wait_send()
    for step in range(n - 1):
        for way in range(2):
            @pl.when(q_sends(way, step))
            def _():
                for h in range(PIECES):
                    q_copy(way, step, h).wait_send()
    for o in range(1, n):
        stats_copy(lax.rem(z + o, n)).wait_send()


def local(sizes, queries, passages, head_weight, positives, negative_ids, negative_count):
    n, shards, pairs, max_list = sizes
    towers = shards // CORES
    width = queries.shape[2]
    rows_p = passages.shape[1]
    meta_rows = -(-(max_list + 1) // 8) * 8
    hops = max(n - 1, 1)
    dma = pltpu.SemaphoreType.DMA
    far = max(towers - 1, 1)
    return pl.pallas_call(
        functools.partial(kernel, sizes),
        out_shape=jax.ShapeDtypeStruct((1, BLOCK), jnp.float32),
        in_specs=[
            pl.BlockSpec(memory_space=pltpu.HBM),
        ] * 6,
        out_specs=pl.BlockSpec(memory_space=pltpu.VMEM),
        scratch_shapes=[
            pltpu.VMEM((n, BLOCK, width), jnp.bfloat16),
            pltpu.VMEM((pairs * rows_p, width), jnp.bfloat16),
            pltpu.VMEM((pairs * rows_p, width), jnp.bfloat16),
            pltpu.VMEM((shards * head_weight.shape[0], width), jnp.bfloat16),
            pltpu.VMEM((n, meta_rows, BLOCK), jnp.int32),
            pltpu.VMEM((n, 8, BLOCK), jnp.float32),
            pltpu.VMEM((n, 8, BLOCK), jnp.float32),
            pltpu.SMEM(negative_ids.shape, jnp.int32),
            pltpu.SMEM(negative_count.shape, jnp.int32),
            pltpu.VMEM((pairs * rows_p, width), jnp.float32),
            pltpu.VMEM((3, BLOCK, width), jnp.float32),
            pltpu.VMEM((BLOCK, width), jnp.bfloat16),
            dma((6,)),
            dma((2, hops, PIECES)), dma((2, hops, PIECES)),
            dma((max(pairs - 1, 1), PIECES)), dma((max(pairs - 1, 1), PIECES)),
            dma, dma,
            dma((far, PIECES)), dma((far, PIECES)),
            dma((far, PIECES)), dma((far, PIECES)),
            dma((hops,)), dma((hops,)),
            dma((n,)), dma((n,)),
        ],
        compiler_params=pltpu.CompilerParams(
            collective_id=0, has_side_effects=True, vmem_limit_bytes=64 * 1024 * 1024
        ),
        name="retriever_loss",
    )(queries, passages, head_weight, positives, negative_ids, negative_count)


def solution(mesh):
    in_specs = (
        P("fsdp", ("dp", "query"), None),
        P("fsdp", ("dp", "query"), None),
        P("fsdp", None),
        P("fsdp", ("dp", "query")),
        P("fsdp", ("dp", "query"), None),
        P("fsdp", ("dp", "query")),
    )
    out_specs = P("fsdp", ("dp", "query"))

    def whole(queries, passages, head_weight, positives, negative_ids, negative_count):
        sizes = (
            mesh.shape["dp"], mesh.shape["fsdp"], mesh.shape["query"], negative_ids.shape[2]
        )
        return jax.shard_map(
            functools.partial(local, sizes),
            mesh=mesh, in_specs=in_specs, out_specs=out_specs, check_vma=False,
        )(queries, passages, head_weight, positives, negative_ids, negative_count)

    return whole
```

```python
import functools

import jax
import jax.numpy as jnp
from jax import lax
from jax.experimental import pallas as pl
from jax.experimental.pallas import tpu as pltpu
from jax.sharding import PartitionSpec as P

BLOCK = 128
CORES = 2
PIECES = 2
MASKED = -1e30
MESH = pl.DeviceIdType.MESH


def kernel(
    sizes, q_ref, p_ref, w_ref, pos_ref, ids_ref, count_ref, out_ref,
    q_all, p_all, p_proj, w_all, meta, stats_out, stats_in, ids_own, count_own,
    p_part, q_part, q_proj, p_far, q_far, far_out,
    local_sem, q_send, q_recv, p_send, p_recv, own_send, own_recv,
    wy_send, wy_recv, wc_send, wc_recv, meta_send, meta_recv, st_send, st_recv,
    pf_send, pf_recv, qf_send, qf_recv, mf_send, mf_recv, ex_send, ex_recv,
):
    n, shards, pairs, max_list = sizes
    towers = shards // CORES
    rows_w = w_ref.shape[0]
    rows_p = p_ref.shape[1]
    width = q_ref.shape[2]
    piece_q = BLOCK // PIECES
    piece_w = rows_w // PIECES
    piece_p = rows_p // PIECES
    scale = width ** -0.5
    z = lax.axis_index("dp")
    f = lax.axis_index("fsdp")
    x = lax.axis_index("query")
    core = lax.rem(f, CORES)
    mate = f + 1 - 2 * core

    short = n == 4 and pairs == 2
    folded = (core == 1) if short else False
    outer = (z == 0) | (z == n - 1)
    far = lax.rem(z + 2, n)
    beside = z + 1 - 2 * lax.rem(z, 2)
    across = lax.rem(x + 1, pairs)
    slots = n + 2 if short else n

    def remote(src, dst, send, recv, where):
        return pltpu.make_async_remote_copy(
            src_ref=src, dst_ref=dst, send_sem=send, recv_sem=recv,
            device_id=where, device_id_type=MESH,
        )

    def shard_rows(shard, c):
        start = pl.multiple_of(shard * rows_w + c * piece_w, piece_w)
        return w_all.at[pl.ds(start, piece_w)]

    def p_rows(holder, h):
        return p_all.at[p_piece(holder, h)]

    def p_piece(holder, h):
        return pl.ds(pl.multiple_of(holder * rows_p + h * piece_p, piece_p), piece_p)

    own_w = w_all.at[pl.ds(pl.multiple_of(f * rows_w, rows_w), rows_w)]
    own_p = p_all.at[pl.ds(pl.multiple_of(x * rows_p, rows_p), rows_p)]
    lists_ = [
        pltpu.make_async_copy(pos_ref, meta.at[z, pl.ds(0, 1)], local_sem.at[3]),
        pltpu.make_async_copy(ids_ref, ids_own, local_sem.at[4]),
        pltpu.make_async_copy(count_ref, count_own, local_sem.at[5]),
    ]
    for copy in lists_:
        copy.start()
    locals_ = [
        pltpu.make_async_copy(w_ref, own_w, local_sem.at[0]),
        pltpu.make_async_copy(p_ref.at[0], own_p, local_sem.at[1]),
        pltpu.make_async_copy(q_ref.at[0], q_all.at[z], local_sem.at[2]),
    ]
    for copy in locals_:
        copy.start()

    barrier = pltpu.get_barrier_semaphore()
    friends = [{"dp": lax.rem(z + o, n)} for o in range(1, n)]
    friends += [{"query": lax.rem(x + o, pairs)} for o in range(1, pairs)]
    friends += [{"fsdp": lax.rem(f + CORES * o, shards)} for o in range(1, towers)]
    friends += [{"fsdp": mate}]
    if short:
        friends += [{"dp": far, "query": across}]
    for i in range(slots):
        stats_in[i, 0:1, :] = jnp.full((1, BLOCK), MASKED, jnp.float32)
        stats_in[i, 1:3, :] = jnp.zeros((2, BLOCK), jnp.float32)
    for friend in friends:
        pl.semaphore_signal(barrier, inc=1, device_id=friend, device_id_type=MESH)

    for copy in lists_:
        copy.wait()
    live = count_own[0, 0]
    for l in range(max_list):
        entry = jnp.where(l < live, ids_own[0, 0, l], -1)
        meta[z, l + 1:l + 2, :] = jnp.full((1, BLOCK), entry, jnp.int32)
    pl.semaphore_wait(barrier, len(friends))

    def q_copy(way, step, h):
        block = z - step if way == 0 else z + step
        block = jnp.clip(block, 0, n - 1)
        view = q_all.at[block, pl.ds(h * piece_q, piece_q)]
        src = q_ref.at[0, pl.ds(h * piece_q, piece_q)] if step == 0 else view
        target = jnp.minimum(z + 1, n - 1) if way == 0 else jnp.maximum(z - 1, 0)
        return remote(src, view, q_send.at[way, step, h], q_recv.at[way, step, h], {"dp": target})

    def q_sends(way, step):
        there = (z + 1 < n) & (z >= step) if way == 0 else (z >= 1) & (z + step < n)
        return there & jnp.logical_not(folded) if short and step == n - 2 else there

    def q_wait(way, step, h):
        block = z - 1 - step if way == 0 else z + 1 + step
        block = jnp.clip(block, 0, n - 1)
        view = q_all.at[block, pl.ds(h * piece_q, piece_q)]
        pltpu.make_async_copy(view, view, q_recv.at[way, step, h]).wait()

    def q_receives(way, step):
        return z - 1 - step >= 0 if way == 0 else z + 1 + step < n

    def qf_copy(h):
        part = pl.ds(h * piece_q, piece_q)
        return remote(
            q_all.at[far, part], q_far.at[part], qf_send.at[h], qf_recv.at[h], {"query": across}
        )

    def pf_copy():
        return remote(p_ref.at[0], p_far, pf_send, pf_recv, {"dp": beside})

    def mf_copy():
        return remote(meta.at[z], meta.at[n], mf_send, mf_recv, {"dp": far, "query": across})

    def ex_copy(i):
        where = {"dp": far, "query": across} if i else {"dp": far}
        return remote(far_out.at[i], stats_in.at[n + i], ex_send.at[i], ex_recv.at[i], where)

    for h in range(PIECES):
        for way in range(2):
            @pl.when(q_sends(way, 0))
            def _():
                q_copy(way, 0, h).start()

    sent = []
    for c in range(PIECES):
        for o in range(1, towers):
            copy = remote(
                w_ref.at[pl.ds(c * piece_w, piece_w)], shard_rows(f, c),
                wy_send.at[o - 1, c], wy_recv.at[o - 1, c],
                {"fsdp": lax.rem(f + CORES * o, shards)},
            )
            copy.start()
            sent.append(copy)
    for h in range(PIECES):
        for o in range(1, pairs):
            copy = remote(
                p_ref.at[0, pl.ds(h * piece_p, piece_p)], p_rows(x, h),
                p_send.at[o - 1, h], p_recv.at[o - 1, h], {"query": lax.rem(x + o, pairs)},
            )
            copy.start()
            sent.append(copy)
    if short:
        @pl.when(folded & outer)
        def _():
            pf_copy().start()
            mf_copy().start()
    own_copy = remote(w_ref, own_w, own_send, own_recv, {"fsdp": mate})
    own_copy.start()
    sent.append(own_copy)
    for o in range(1, n):
        copy = remote(
            meta.at[z], meta.at[z], meta_send.at[o - 1], meta_recv.at[o - 1],
            {"dp": lax.rem(z + o, n)},
        )
        copy.start()
        sent.append(copy)

    def pass_queries(step, h):
        for way in range(2):
            @pl.when(q_receives(way, step))
            def _():
                q_wait(way, step, h)

            @pl.when(q_sends(way, step + 1))
            def _():
                q_copy(way, step + 1, h).start()

        if short and step == 1:
            @pl.when(folded & jnp.logical_not(outer))
            def _():
                qf_copy(h).start()

    def pass_weights(c):
        for o in range(1, towers):
            shard = lax.rem(f + shards - CORES * o, shards)
            view = shard_rows(shard, c)
            pltpu.make_async_copy(view, view, wy_recv.at[o - 1, c]).wait()
            copy = remote(view, view, wc_send.at[o - 1, c], wc_recv.at[o - 1, c], {"fsdp": mate})
            copy.start()
            sent.append(copy)

    def span(shard, c, depth):
        return pl.ds(pl.multiple_of(shard * rows_w + c * piece_w, depth), depth)

    fine = piece_w % 128 == 0
    towers_from = [lax.rem(f - core + CORES * o, shards) for o in range(1, towers)]
    first_spans = [span(f - core, 0, CORES * rows_w)]
    if fine:
        piece_spans = [
            [span(base + k, c, piece_w) for base in towers_from for k in range(CORES)]
            for c in range(PIECES)
        ]
        last_spans = [one for c in range(1, PIECES) for one in piece_spans[c]]
    else:
        last_spans = [span(base, 0, CORES * rows_w) for base in towers_from]

    def partly(rows, spans):
        lhs = [rows[:, one] for one in spans]
        rhs = [w_all[one, :] for one in spans]
        lhs = lhs[0] if len(lhs) == 1 else jnp.concatenate(lhs, axis=1)
        rhs = rhs[0] if len(rhs) == 1 else jnp.concatenate(rhs, axis=0)
        return jnp.dot(lhs, rhs, preferred_element_type=jnp.float32)

    def project(rows):
        return jnp.dot(rows, w_all[...], preferred_element_type=jnp.float32).astype(jnp.bfloat16)

    def mate_weights(c):
        for o in range(1, towers):
            view = shard_rows(lax.rem(mate + shards - CORES * o, shards), c)
            pltpu.make_async_copy(view, view, wc_recv.at[o - 1, c]).wait()

    def neighbours(act):
        for way in range(2):
            @pl.when(q_receives(way, 0))
            def _():
                act(q_all.at[z - 1 if way == 0 else z + 1], q_part.at[1 + way])

    def begin(rows, part):
        part[...] = partly(rows, first_spans)

    def extend(rows, part):
        part[...] += partly(rows, piece_spans[0])

    own_part = p_part.at[pl.ds(pl.multiple_of(x * rows_p, rows_p), rows_p)]
    for copy in locals_:
        copy.wait()
    other_w = w_all.at[pl.ds(pl.multiple_of(mate * rows_w, rows_w), rows_w)]
    pltpu.make_async_copy(other_w, other_w, own_recv).wait()
    begin(own_p, own_part)
    begin(q_all.at[z], q_part.at[0])
    pass_queries(0, 0)
    pass_weights(0)
    pass_queries(0, 1)
    neighbours(begin)
    mate_weights(0)
    if fine:
        extend(own_p, own_part)
        extend(q_all.at[z], q_part.at[0])
        neighbours(extend)
    for o in range(1, pairs):
        holder = lax.rem(x + pairs - o, pairs)
        view = p_rows(holder, 0)
        pltpu.make_async_copy(view, view, p_recv.at[o - 1, 0]).wait()
        p_part[p_piece(holder, 0), :] = partly(
            view, first_spans + piece_spans[0] if fine else first_spans
        )
    for step in range(1, n - 2):
        pass_queries(step, 0)
        if step == 1:
            pass_weights(1)
        pass_queries(step, 1)
    mate_weights(1)

    for o in range(pairs):
        holder = lax.rem(x + pairs - o, pairs)
        for h in range(PIECES):
            view = p_rows(holder, h)
            piece = p_piece(holder, h)
            if o and h:
                pltpu.make_async_copy(view, view, p_recv.at[o - 1, h]).wait()
                p_proj[piece, :] = project(view[...])
            else:
                whole = p_part[piece, :] + partly(view, last_spans)
                p_proj[piece, :] = whole.astype(jnp.bfloat16)

    for o in range(1, n):
        view = meta.at[lax.rem(z + n - o, n)]
        pltpu.make_async_copy(view, view, meta_recv.at[o - 1]).wait()

    tiles = pairs * rows_p // BLOCK
    first_tile = z * tiles
    row_index = lax.broadcasted_iota(jnp.int32, (BLOCK, BLOCK), 0)

    def stats_copy(block):
        return remote(
            stats_out.at[block], stats_in.at[z], st_send.at[block], st_recv.at[z], {"dp": block}
        )

    def block_stats(held, info, tile_id):
        logits = lax.dot_general(
            held, q_proj[...], (((1,), (1,)), ((), ())), preferred_element_type=jnp.float32
        ) * scale
        target = info[0:1, :]
        top = jnp.full((1, BLOCK), MASKED, jnp.float32)
        target_logit = jnp.zeros((1, BLOCK), jnp.float32)
        picks = []
        for k in range(held.shape[0] // BLOCK):
            tile = logits[k * BLOCK:(k + 1) * BLOCK, :]
            listed = info[1:2, :] == tile_id + k
            for l in range(1, max_list):
                listed = listed | (info[l + 1:l + 2, :] == tile_id + k)
            is_target = row_index == target - (tile_id + k) * BLOCK
            chosen = listed | is_target
            picks.append((tile, chosen))
            top = jnp.maximum(
                top, jnp.max(jnp.where(chosen, tile, MASKED), axis=0, keepdims=True)
            )
            target_logit += jnp.sum(jnp.where(is_target, tile, 0.0), axis=0, keepdims=True)
        total = jnp.zeros((1, BLOCK), jnp.float32)
        for tile, chosen in picks:
            total += jnp.sum(jnp.where(chosen, jnp.exp(tile - top), 0.0), axis=0, keepdims=True)
        return top, total, target_logit

    def far_stats(i, info):
        found = block_stats(p_far[...], info, beside * tiles + x * (rows_p // BLOCK))
        for j in range(3):
            far_out[i, j:j + 1, :] = found[j]
        ex_copy(i).start()

    if short:
        @pl.when(folded & jnp.logical_not(outer))
        def _():
            pltpu.make_async_copy(p_far, p_far, pf_recv).wait()
            p_far[...] = project(p_far[...])

    def meet(t, carry):
        away = lax.div(t + 1, 2)
        way = lax.rem(t + 1, 2)
        place = jnp.where(way == 0, z - away, z + away)
        block = jnp.clip(place, 0, n - 1)

        meets = (place >= 0) & (place < n)
        if short:
            meets = meets & jnp.logical_not(folded & (away == n - 1))

        @pl.when(meets)
        def _():
            @pl.when(away <= 1)
            def _():
                rest = partly(q_all.at[block], last_spans)
                q_proj[...] = (q_part[jnp.minimum(t, 2)] + rest).astype(jnp.bfloat16)

            @pl.when((away > 1) & (away < n - 1))
            def _():
                q_proj[...] = project(q_all[block])

            @pl.when(away == n - 1)
            def _():
                for h in range(PIECES):
                    part = pl.ds(h * piece_q, piece_q)
                    view = q_all.at[block, part]
                    pltpu.make_async_copy(view, view, q_recv.at[way, n - 2, h]).wait()
                    q_proj[part, :] = project(view[...])

            top, total, target_logit = block_stats(p_proj[...], meta[block], first_tile)

            @pl.when(t == 0)
            def _():
                stats_in[z, 0:1, :] = top
                stats_in[z, 1:2, :] = total
                stats_in[z, 2:3, :] = target_logit

            @pl.when(t > 0)
            def _():
                stats_out[block, 0:1, :] = top
                stats_out[block, 1:2, :] = total
                stats_out[block, 2:3, :] = target_logit
                stats_copy(block).start()

            if short:
                @pl.when(folded & jnp.logical_not(outer) & (away == 2))
                def _():
                    far_stats(0, meta[block])

        return carry

    lax.fori_loop(0, 2 * n - 1, meet, 0)

    if short:
        @pl.when(folded & jnp.logical_not(outer))
        def _():
            for h in range(PIECES):
                view = q_far.at[pl.ds(h * piece_q, piece_q)]
                pltpu.make_async_copy(view, view, qf_recv.at[h]).wait()
            view = meta.at[n]
            pltpu.make_async_copy(view, view, mf_recv).wait()
            q_proj[...] = project(q_far[...])
            far_stats(1, meta[n])

    def reaches(other):
        ends = (z + other == n - 1) & outer
        return jnp.logical_not(folded & ends) if short else other >= 0

    for o in range(1, n):
        other = lax.rem(z + o, n)

        @pl.when(reaches(other))
        def _():
            view = stats_in.at[other]
            pltpu.make_async_copy(view, view, st_recv.at[other]).wait()

    if short:
        @pl.when(folded & outer)
        def _():
            for i in range(2):
                view = stats_in.at[n + i]
                pltpu.make_async_copy(view, view, ex_recv.at[i]).wait()
    top = stats_in[0, 0:1, :]
    for i in range(1, slots):
        top = jnp.maximum(top, stats_in[i, 0:1, :])
    total = jnp.zeros((1, BLOCK), jnp.float32)
    target_logit = jnp.zeros((1, BLOCK), jnp.float32)
    for i in range(slots):
        total += stats_in[i, 1:2, :] * jnp.exp(stats_in[i, 0:1, :] - top)
        target_logit += stats_in[i, 2:3, :]
    out_ref[...] = top + jnp.log(total) - target_logit

    for copy in sent:
        copy.wait_send()
    for step in range(n - 1):
        for way in range(2):
            @pl.when(q_sends(way, step))
            def _():
                for h in range(PIECES):
                    q_copy(way, step, h).wait_send()
    for o in range(1, n):
        other = lax.rem(z + o, n)

        @pl.when(reaches(other))
        def _():
            stats_copy(other).wait_send()
    if short:
        @pl.when(folded & outer)
        def _():
            pf_copy().wait_send()
            mf_copy().wait_send()

        @pl.when(folded & jnp.logical_not(outer))
        def _():
            for h in range(PIECES):
                qf_copy(h).wait_send()
            for i in range(2):
                ex_copy(i).wait_send()


def local(sizes, queries, passages, head_weight, positives, negative_ids, negative_count):
    n, shards, pairs, max_list = sizes
    towers = shards // CORES
    width = queries.shape[2]
    rows_p = passages.shape[1]
    meta_rows = -(-(max_list + 1) // 8) * 8
    hops = max(n - 1, 1)
    dma = pltpu.SemaphoreType.DMA
    far = max(towers - 1, 1)
    return pl.pallas_call(
        functools.partial(kernel, sizes),
        out_shape=jax.ShapeDtypeStruct((1, BLOCK), jnp.float32),
        in_specs=[
            pl.BlockSpec(memory_space=pltpu.HBM),
        ] * 6,
        out_specs=pl.BlockSpec(memory_space=pltpu.VMEM),
        scratch_shapes=[
            pltpu.VMEM((n, BLOCK, width), jnp.bfloat16),
            pltpu.VMEM((pairs * rows_p, width), jnp.bfloat16),
            pltpu.VMEM((pairs * rows_p, width), jnp.bfloat16),
            pltpu.VMEM((shards * head_weight.shape[0], width), jnp.bfloat16),
            pltpu.VMEM((n + 1, meta_rows, BLOCK), jnp.int32),
            pltpu.VMEM((n, 8, BLOCK), jnp.float32),
            pltpu.VMEM((n + 2, 8, BLOCK), jnp.float32),
            pltpu.SMEM(negative_ids.shape, jnp.int32),
            pltpu.SMEM(negative_count.shape, jnp.int32),
            pltpu.VMEM((pairs * rows_p, width), jnp.float32),
            pltpu.VMEM((3, BLOCK, width), jnp.float32),
            pltpu.VMEM((BLOCK, width), jnp.bfloat16),
            pltpu.VMEM((rows_p, width), jnp.bfloat16),
            pltpu.VMEM((BLOCK, width), jnp.bfloat16),
            pltpu.VMEM((2, 8, BLOCK), jnp.float32),
            dma((6,)),
            dma((2, hops, PIECES)), dma((2, hops, PIECES)),
            dma((max(pairs - 1, 1), PIECES)), dma((max(pairs - 1, 1), PIECES)),
            dma, dma,
            dma((far, PIECES)), dma((far, PIECES)),
            dma((far, PIECES)), dma((far, PIECES)),
            dma((hops,)), dma((hops,)),
            dma((n,)), dma((n,)),
            dma, dma, dma((PIECES,)), dma((PIECES,)), dma, dma, dma((2,)), dma((2,)),
        ],
        compiler_params=pltpu.CompilerParams(
            collective_id=0, has_side_effects=True, vmem_limit_bytes=64 * 1024 * 1024
        ),
        name="retriever_loss",
    )(queries, passages, head_weight, positives, negative_ids, negative_count)


def solution(mesh):
    in_specs = (
        P("fsdp", ("dp", "query"), None),
        P("fsdp", ("dp", "query"), None),
        P("fsdp", None),
        P("fsdp", ("dp", "query")),
        P("fsdp", ("dp", "query"), None),
        P("fsdp", ("dp", "query")),
    )
    out_specs = P("fsdp", ("dp", "query"))

    def whole(queries, passages, head_weight, positives, negative_ids, negative_count):
        sizes = (
            mesh.shape["dp"], mesh.shape["fsdp"], mesh.shape["query"], negative_ids.shape[2]
        )
        return jax.shard_map(
            functools.partial(local, sizes),
            mesh=mesh, in_specs=in_specs, out_specs=out_specs, check_vma=False,
        )(queries, passages, head_weight, positives, negative_ids, negative_count)

    return whole
```

```python
import functools

import jax
import jax.numpy as jnp
from jax import lax
from jax.experimental import pallas as pl
from jax.experimental.pallas import tpu as pltpu
from jax.sharding import PartitionSpec as P

BLOCK = 128
CORES = 2
PIECES = 2
MASKED = -1e30
MESH = pl.DeviceIdType.MESH


def kernel(
    sizes, q_ref, p_ref, w_ref, pos_ref, ids_ref, count_ref, out_ref,
    q_all, p_all, p_proj, w_all, meta, stats_out, stats_in, ids_own, count_own,
    p_part, q_part, q_proj,
    local_sem, q_send, q_recv, p_send, p_recv, own_send, own_recv,
    wy_send, wy_recv, wc_send, wc_recv, meta_send, meta_recv, st_send, st_recv,
):
    n, shards, pairs, max_list = sizes
    towers = shards // CORES
    rows_w = w_ref.shape[0]
    rows_p = p_ref.shape[1]
    width = q_ref.shape[2]
    piece_q = BLOCK // PIECES
    piece_w = rows_w // PIECES
    piece_p = rows_p // PIECES
    scale = width ** -0.5
    z = lax.axis_index("dp")
    f = lax.axis_index("fsdp")
    x = lax.axis_index("query")
    core = lax.rem(f, CORES)
    mate = f + 1 - 2 * core

    def remote(src, dst, send, recv, where):
        return pltpu.make_async_remote_copy(
            src_ref=src, dst_ref=dst, send_sem=send, recv_sem=recv,
            device_id=where, device_id_type=MESH,
        )

    def shard_rows(shard, c):
        start = pl.multiple_of(shard * rows_w + c * piece_w, piece_w)
        return w_all.at[pl.ds(start, piece_w)]

    def p_rows(holder, h):
        return p_all.at[p_piece(holder, h)]

    def p_piece(holder, h):
        return pl.ds(pl.multiple_of(holder * rows_p + h * piece_p, piece_p), piece_p)

    own_w = w_all.at[pl.ds(pl.multiple_of(f * rows_w, rows_w), rows_w)]
    own_p = p_all.at[pl.ds(pl.multiple_of(x * rows_p, rows_p), rows_p)]
    lists_ = [
        pltpu.make_async_copy(pos_ref, meta.at[z, pl.ds(0, 1)], local_sem.at[3]),
        pltpu.make_async_copy(ids_ref, ids_own, local_sem.at[4]),
        pltpu.make_async_copy(count_ref, count_own, local_sem.at[5]),
    ]
    for copy in lists_:
        copy.start()
    locals_ = [
        pltpu.make_async_copy(w_ref, own_w, local_sem.at[0]),
        pltpu.make_async_copy(p_ref.at[0], own_p, local_sem.at[1]),
        pltpu.make_async_copy(q_ref.at[0], q_all.at[z], local_sem.at[2]),
    ]
    for copy in locals_:
        copy.start()

    barrier = pltpu.get_barrier_semaphore()
    friends = [{"dp": lax.rem(z + o, n)} for o in range(1, n)]
    friends += [{"query": lax.rem(x + o, pairs)} for o in range(1, pairs)]
    friends += [{"fsdp": lax.rem(f + CORES * o, shards)} for o in range(1, towers)]
    friends += [{"fsdp": mate}]
    for friend in friends:
        pl.semaphore_signal(barrier, inc=1, device_id=friend, device_id_type=MESH)

    for copy in lists_:
        copy.wait()
    live = count_own[0, 0]
    for l in range(max_list):
        entry = jnp.where(l < live, ids_own[0, 0, l], -1)
        meta[z, l + 1:l + 2, :] = jnp.full((1, BLOCK), entry, jnp.int32)
    pl.semaphore_wait(barrier, len(friends))

    def q_copy(way, step, h):
        block = z - step if way == 0 else z + step
        block = jnp.clip(block, 0, n - 1)
        view = q_all.at[block, pl.ds(h * piece_q, piece_q)]
        src = q_ref.at[0, pl.ds(h * piece_q, piece_q)] if step == 0 else view
        target = jnp.minimum(z + 1, n - 1) if way == 0 else jnp.maximum(z - 1, 0)
        return remote(src, view, q_send.at[way, step, h], q_recv.at[way, step, h], {"dp": target})

    def q_sends(way, step):
        if way == 0:
            return (z + 1 < n) & (z >= step)
        return (z >= 1) & (z + step < n)

    def q_wait(way, step, h):
        block = z - 1 - step if way == 0 else z + 1 + step
        block = jnp.clip(block, 0, n - 1)
        view = q_all.at[block, pl.ds(h * piece_q, piece_q)]
        pltpu.make_async_copy(view, view, q_recv.at[way, step, h]).wait()

    def q_receives(way, step):
        return z - 1 - step >= 0 if way == 0 else z + 1 + step < n

    for h in range(PIECES):
        for way in range(2):
            @pl.when(q_sends(way, 0))
            def _():
                q_copy(way, 0, h).start()

    sent = []
    for c in range(PIECES):
        for o in range(1, towers):
            copy = remote(
                w_ref.at[pl.ds(c * piece_w, piece_w)], shard_rows(f, c),
                wy_send.at[o - 1, c], wy_recv.at[o - 1, c],
                {"fsdp": lax.rem(f + CORES * o, shards)},
            )
            copy.start()
            sent.append(copy)
    for h in range(PIECES):
        for o in range(1, pairs):
            copy = remote(
                p_ref.at[0, pl.ds(h * piece_p, piece_p)], p_rows(x, h),
                p_send.at[o - 1, h], p_recv.at[o - 1, h], {"query": lax.rem(x + o, pairs)},
            )
            copy.start()
            sent.append(copy)
    own_copy = remote(w_ref, own_w, own_send, own_recv, {"fsdp": mate})
    own_copy.start()
    sent.append(own_copy)
    for o in range(1, n):
        copy = remote(
            meta.at[z], meta.at[z], meta_send.at[o - 1], meta_recv.at[o - 1],
            {"dp": lax.rem(z + o, n)},
        )
        copy.start()
        sent.append(copy)

    def pass_queries(step, h):
        for way in range(2):
            @pl.when(q_receives(way, step))
            def _():
                q_wait(way, step, h)

            @pl.when(q_sends(way, step + 1))
            def _():
                q_copy(way, step + 1, h).start()

    def pass_weights(c):
        for o in range(1, towers):
            shard = lax.rem(f + shards - CORES * o, shards)
            view = shard_rows(shard, c)
            pltpu.make_async_copy(view, view, wy_recv.at[o - 1, c]).wait()
            copy = remote(view, view, wc_send.at[o - 1, c], wc_recv.at[o - 1, c], {"fsdp": mate})
            copy.start()
            sent.append(copy)

    def span(shard, c, depth):
        return pl.ds(pl.multiple_of(shard * rows_w + c * piece_w, depth), depth)

    towers_from = [lax.rem(f - core + CORES * o, shards) for o in range(1, towers)]
    first_spans = [span(f - core, 0, CORES * rows_w)]
    last_spans = [span(base, 0, CORES * rows_w) for base in towers_from]

    def partly(rows, spans):
        lhs = [rows[:, one] for one in spans]
        rhs = [w_all[one, :] for one in spans]
        lhs = lhs[0] if len(lhs) == 1 else jnp.concatenate(lhs, axis=1)
        rhs = rhs[0] if len(rhs) == 1 else jnp.concatenate(rhs, axis=0)
        return jnp.dot(lhs, rhs, preferred_element_type=jnp.float32)

    def project(rows):
        return jnp.dot(rows, w_all[...], preferred_element_type=jnp.float32).astype(jnp.bfloat16)

    def mate_weights(c):
        for o in range(1, towers):
            view = shard_rows(lax.rem(mate + shards - CORES * o, shards), c)
            pltpu.make_async_copy(view, view, wc_recv.at[o - 1, c]).wait()

    def neighbours(act):
        for way in range(2):
            @pl.when(q_receives(way, 0))
            def _():
                act(q_all.at[z - 1 if way == 0 else z + 1], q_part.at[1 + way])

    def begin(rows, part):
        part[...] = partly(rows, first_spans)

    own_part = p_part.at[pl.ds(pl.multiple_of(x * rows_p, rows_p), rows_p)]
    for copy in locals_:
        copy.wait()
    other_w = w_all.at[pl.ds(pl.multiple_of(mate * rows_w, rows_w), rows_w)]
    pltpu.make_async_copy(other_w, other_w, own_recv).wait()
    begin(own_p, own_part)
    begin(q_all.at[z], q_part.at[0])
    pass_queries(0, 0)
    pass_queries(0, 1)
    neighbours(begin)
    for step in range(1, n - 2):
        pass_queries(step, 0)
        if step == 1:
            pass_weights(0)
        pass_queries(step, 1)
    pass_weights(1)
    mate_weights(0)
    mate_weights(1)

    for o in range(pairs):
        holder = lax.rem(x + pairs - o, pairs)
        for h in range(PIECES):
            view = p_rows(holder, h)
            piece = p_piece(holder, h)
            if o:
                pltpu.make_async_copy(view, view, p_recv.at[o - 1, h]).wait()
                p_proj[piece, :] = project(view[...])
            else:
                whole = p_part[piece, :] + partly(view, last_spans)
                p_proj[piece, :] = whole.astype(jnp.bfloat16)

    for o in range(1, n):
        view = meta.at[lax.rem(z + n - o, n)]
        pltpu.make_async_copy(view, view, meta_recv.at[o - 1]).wait()

    tiles = pairs * rows_p // BLOCK
    first_tile = z * tiles
    row_index = lax.broadcasted_iota(jnp.int32, (BLOCK, BLOCK), 0)

    def stats_copy(block):
        return remote(
            stats_out.at[block], stats_in.at[z], st_send.at[block], st_recv.at[z], {"dp": block}
        )

    def meet(t, carry):
        away = lax.div(t + 1, 2)
        way = lax.rem(t + 1, 2)
        place = jnp.where(way == 0, z - away, z + away)
        block = jnp.clip(place, 0, n - 1)

        @pl.when((place >= 0) & (place < n))
        def _():
            @pl.when(away <= 1)
            def _():
                rest = partly(q_all.at[block], last_spans)
                q_proj[...] = (q_part[jnp.minimum(t, 2)] + rest).astype(jnp.bfloat16)

            @pl.when((away > 1) & (away < n - 1))
            def _():
                q_proj[...] = project(q_all[block])

            @pl.when(away == n - 1)
            def _():
                for h in range(PIECES):
                    part = pl.ds(h * piece_q, piece_q)
                    view = q_all.at[block, part]
                    pltpu.make_async_copy(view, view, q_recv.at[way, n - 2, h]).wait()
                    q_proj[part, :] = project(view[...])

            logits = lax.dot_general(
                p_proj[...], q_proj[...], (((1,), (1,)), ((), ())),
                preferred_element_type=jnp.float32,
            ) * scale
            info = meta[block]
            target = info[0:1, :]
            top = jnp.full((1, BLOCK), MASKED, jnp.float32)
            target_logit = jnp.zeros((1, BLOCK), jnp.float32)
            picks = []
            for k in range(tiles):
                tile = logits[k * BLOCK:(k + 1) * BLOCK, :]
                listed = info[1:2, :] == first_tile + k
                for l in range(1, max_list):
                    listed = listed | (info[l + 1:l + 2, :] == first_tile + k)
                is_target = row_index == target - (first_tile + k) * BLOCK
                chosen = listed | is_target
                picks.append((tile, chosen))
                top = jnp.maximum(
                    top, jnp.max(jnp.where(chosen, tile, MASKED), axis=0, keepdims=True)
                )
                target_logit += jnp.sum(jnp.where(is_target, tile, 0.0), axis=0, keepdims=True)
            total = jnp.zeros((1, BLOCK), jnp.float32)
            for tile, chosen in picks:
                total += jnp.sum(
                    jnp.where(chosen, jnp.exp(tile - top), 0.0), axis=0, keepdims=True
                )

            @pl.when(t == 0)
            def _():
                stats_in[z, 0:1, :] = top
                stats_in[z, 1:2, :] = total
                stats_in[z, 2:3, :] = target_logit

            @pl.when(t > 0)
            def _():
                stats_out[block, 0:1, :] = top
                stats_out[block, 1:2, :] = total
                stats_out[block, 2:3, :] = target_logit
                stats_copy(block).start()

        return carry

    lax.fori_loop(0, 2 * n - 1, meet, 0)

    for o in range(1, n):
        view = stats_in.at[lax.rem(z + o, n)]
        pltpu.make_async_copy(view, view, st_recv.at[lax.rem(z + o, n)]).wait()
    top = stats_in[0, 0:1, :]
    for i in range(1, n):
        top = jnp.maximum(top, stats_in[i, 0:1, :])
    total = jnp.zeros((1, BLOCK), jnp.float32)
    target_logit = jnp.zeros((1, BLOCK), jnp.float32)
    for i in range(n):
        total += stats_in[i, 1:2, :] * jnp.exp(stats_in[i, 0:1, :] - top)
        target_logit += stats_in[i, 2:3, :]
    out_ref[...] = top + jnp.log(total) - target_logit

    for copy in sent:
        copy.wait_send()
    for step in range(n - 1):
        for way in range(2):
            @pl.when(q_sends(way, step))
            def _():
                for h in range(PIECES):
                    q_copy(way, step, h).wait_send()
    for o in range(1, n):
        stats_copy(lax.rem(z + o, n)).wait_send()


def local(sizes, queries, passages, head_weight, positives, negative_ids, negative_count):
    n, shards, pairs, max_list = sizes
    towers = shards // CORES
    width = queries.shape[2]
    rows_p = passages.shape[1]
    meta_rows = -(-(max_list + 1) // 8) * 8
    hops = max(n - 1, 1)
    dma = pltpu.SemaphoreType.DMA
    far = max(towers - 1, 1)
    return pl.pallas_call(
        functools.partial(kernel, sizes),
        out_shape=jax.ShapeDtypeStruct((1, BLOCK), jnp.float32),
        in_specs=[
            pl.BlockSpec(memory_space=pltpu.HBM),
        ] * 6,
        out_specs=pl.BlockSpec(memory_space=pltpu.VMEM),
        scratch_shapes=[
            pltpu.VMEM((n, BLOCK, width), jnp.bfloat16),
            pltpu.VMEM((pairs * rows_p, width), jnp.bfloat16),
            pltpu.VMEM((pairs * rows_p, width), jnp.bfloat16),
            pltpu.VMEM((shards * head_weight.shape[0], width), jnp.bfloat16),
            pltpu.VMEM((n, meta_rows, BLOCK), jnp.int32),
            pltpu.VMEM((n, 8, BLOCK), jnp.float32),
            pltpu.VMEM((n, 8, BLOCK), jnp.float32),
            pltpu.SMEM(negative_ids.shape, jnp.int32),
            pltpu.SMEM(negative_count.shape, jnp.int32),
            pltpu.VMEM((pairs * rows_p, width), jnp.float32),
            pltpu.VMEM((3, BLOCK, width), jnp.float32),
            pltpu.VMEM((BLOCK, width), jnp.bfloat16),
            dma((6,)),
            dma((2, hops, PIECES)), dma((2, hops, PIECES)),
            dma((max(pairs - 1, 1), PIECES)), dma((max(pairs - 1, 1), PIECES)),
            dma, dma,
            dma((far, PIECES)), dma((far, PIECES)),
            dma((far, PIECES)), dma((far, PIECES)),
            dma((hops,)), dma((hops,)),
            dma((n,)), dma((n,)),
        ],
        compiler_params=pltpu.CompilerParams(
            collective_id=0, has_side_effects=True, vmem_limit_bytes=64 * 1024 * 1024
        ),
        name="retriever_loss",
    )(queries, passages, head_weight, positives, negative_ids, negative_count)


def solution(mesh):
    in_specs = (
        P("fsdp", ("dp", "query"), None),
        P("fsdp", ("dp", "query"), None),
        P("fsdp", None),
        P("fsdp", ("dp", "query")),
        P("fsdp", ("dp", "query"), None),
        P("fsdp", ("dp", "query")),
    )
    out_specs = P("fsdp", ("dp", "query"))

    def whole(queries, passages, head_weight, positives, negative_ids, negative_count):
        sizes = (
            mesh.shape["dp"], mesh.shape["fsdp"], mesh.shape["query"], negative_ids.shape[2]
        )
        return jax.shard_map(
            functools.partial(local, sizes),
            mesh=mesh, in_specs=in_specs, out_specs=out_specs, check_vma=False,
        )(queries, passages, head_weight, positives, negative_ids, negative_count)

    return whole
```

```python
import functools

import jax
import jax.numpy as jnp
from jax import lax
from jax.experimental import pallas as pl
from jax.experimental.pallas import tpu as pltpu
from jax.sharding import PartitionSpec as P

BLOCK = 128
CORES = 2
PIECES = 2
MASKED = -1e30
MESH = pl.DeviceIdType.MESH


def kernel(
    sizes, q_ref, p_ref, w_ref, pos_ref, ids_ref, count_ref, out_ref,
    q_all, p_all, p_proj, w_all, meta, stats_out, stats_in, ids_own, count_own,
    p_part, q_part, q_proj,
    local_sem, q_send, q_recv, p_send, p_recv, own_send, own_recv,
    wy_send, wy_recv, wc_send, wc_recv, meta_send, meta_recv, st_send, st_recv,
):
    n, shards, pairs, max_list = sizes
    towers = shards // CORES
    rows_w = w_ref.shape[0]
    rows_p = p_ref.shape[1]
    width = q_ref.shape[2]
    piece_q = BLOCK // PIECES
    piece_w = rows_w // PIECES
    piece_p = rows_p // PIECES
    scale = width ** -0.5
    z = lax.axis_index("dp")
    f = lax.axis_index("fsdp")
    x = lax.axis_index("query")
    core = lax.rem(f, CORES)
    mate = f + 1 - 2 * core

    def remote(src, dst, send, recv, where):
        return pltpu.make_async_remote_copy(
            src_ref=src, dst_ref=dst, send_sem=send, recv_sem=recv,
            device_id=where, device_id_type=MESH,
        )

    def shard_rows(shard, c):
        start = pl.multiple_of(shard * rows_w + c * piece_w, piece_w)
        return w_all.at[pl.ds(start, piece_w)]

    def p_rows(holder, h):
        return p_all.at[p_piece(holder, h)]

    def p_piece(holder, h):
        return pl.ds(pl.multiple_of(holder * rows_p + h * piece_p, piece_p), piece_p)

    own_w = w_all.at[pl.ds(pl.multiple_of(f * rows_w, rows_w), rows_w)]
    own_p = p_all.at[pl.ds(pl.multiple_of(x * rows_p, rows_p), rows_p)]
    lists_ = [
        pltpu.make_async_copy(pos_ref, meta.at[z, pl.ds(0, 1)], local_sem.at[3]),
        pltpu.make_async_copy(ids_ref, ids_own, local_sem.at[4]),
        pltpu.make_async_copy(count_ref, count_own, local_sem.at[5]),
    ]
    for copy in lists_:
        copy.start()
    locals_ = [
        pltpu.make_async_copy(w_ref, own_w, local_sem.at[0]),
        pltpu.make_async_copy(p_ref.at[0], own_p, local_sem.at[1]),
        pltpu.make_async_copy(q_ref.at[0], q_all.at[z], local_sem.at[2]),
    ]
    for copy in locals_:
        copy.start()

    barrier = pltpu.get_barrier_semaphore()
    friends = [{"dp": lax.rem(z + o, n)} for o in range(1, n)]
    friends += [{"query": lax.rem(x + o, pairs)} for o in range(1, pairs)]
    friends += [{"fsdp": lax.rem(f + CORES * o, shards)} for o in range(1, towers)]
    friends += [{"fsdp": mate}]
    for friend in friends:
        pl.semaphore_signal(barrier, inc=1, device_id=friend, device_id_type=MESH)

    for copy in lists_:
        copy.wait()
    live = count_own[0, 0]
    for l in range(max_list):
        entry = jnp.where(l < live, ids_own[0, 0, l], -1)
        meta[z, l + 1:l + 2, :] = jnp.full((1, BLOCK), entry, jnp.int32)
    pl.semaphore_wait(barrier, len(friends))

    short = n == 4

    def q_copy(way, step, h):
        if short and step == n - 2:
            part = pl.ds(h * piece_q, piece_q)
            return remote(
                q_ref.at[0, part], q_all.at[z, part],
                q_send.at[way, step, h], q_recv.at[way, step, h], {"dp": (n - 1) - z},
            )
        block = z - step if way == 0 else z + step
        block = jnp.clip(block, 0, n - 1)
        view = q_all.at[block, pl.ds(h * piece_q, piece_q)]
        src = q_ref.at[0, pl.ds(h * piece_q, piece_q)] if step == 0 else view
        target = jnp.minimum(z + 1, n - 1) if way == 0 else jnp.maximum(z - 1, 0)
        return remote(src, view, q_send.at[way, step, h], q_recv.at[way, step, h], {"dp": target})

    def q_sends(way, step):
        if short and step == n - 2:
            return z == 0 if way == 0 else z == n - 1
        if way == 0:
            return (z + 1 < n) & (z >= step)
        return (z >= 1) & (z + step < n)

    def q_wait(way, step, h):
        block = z - 1 - step if way == 0 else z + 1 + step
        block = jnp.clip(block, 0, n - 1)
        view = q_all.at[block, pl.ds(h * piece_q, piece_q)]
        pltpu.make_async_copy(view, view, q_recv.at[way, step, h]).wait()

    def q_receives(way, step):
        return z - 1 - step >= 0 if way == 0 else z + 1 + step < n

    for h in range(PIECES):
        for way in range(2):
            @pl.when(q_sends(way, 0))
            def _():
                q_copy(way, 0, h).start()

    sent = []
    for c in range(PIECES):
        for o in range(1, towers):
            copy = remote(
                w_ref.at[pl.ds(c * piece_w, piece_w)], shard_rows(f, c),
                wy_send.at[o - 1, c], wy_recv.at[o - 1, c],
                {"fsdp": lax.rem(f + CORES * o, shards)},
            )
            copy.start()
            sent.append(copy)
    for h in range(PIECES):
        for o in range(1, pairs):
            copy = remote(
                p_ref.at[0, pl.ds(h * piece_p, piece_p)], p_rows(x, h),
                p_send.at[o - 1, h], p_recv.at[o - 1, h], {"query": lax.rem(x + o, pairs)},
            )
            copy.start()
            sent.append(copy)
    if short:
        for h in range(PIECES):
            for way in range(2):
                @pl.when(q_sends(way, n - 2))
                def _():
                    q_copy(way, n - 2, h).start()
    own_copy = remote(w_ref, own_w, own_send, own_recv, {"fsdp": mate})
    own_copy.start()
    sent.append(own_copy)
    for o in range(1, n):
        copy = remote(
            meta.at[z], meta.at[z], meta_send.at[o - 1], meta_recv.at[o - 1],
            {"dp": lax.rem(z + o, n)},
        )
        copy.start()
        sent.append(copy)

    def pass_queries(step, h):
        for way in range(2):
            @pl.when(q_receives(way, step))
            def _():
                q_wait(way, step, h)

            if not (short and step + 1 == n - 2):
                @pl.when(q_sends(way, step + 1))
                def _():
                    q_copy(way, step + 1, h).start()

    def pass_weights(c):
        for o in range(1, towers):
            shard = lax.rem(f + shards - CORES * o, shards)
            view = shard_rows(shard, c)
            pltpu.make_async_copy(view, view, wy_recv.at[o - 1, c]).wait()
            copy = remote(view, view, wc_send.at[o - 1, c], wc_recv.at[o - 1, c], {"fsdp": mate})
            copy.start()
            sent.append(copy)

    def span(shard, c, depth):
        return pl.ds(pl.multiple_of(shard * rows_w + c * piece_w, depth), depth)

    fine = piece_w % 128 == 0
    towers_from = [lax.rem(f - core + CORES * o, shards) for o in range(1, towers)]
    first_spans = [span(f - core, 0, CORES * rows_w)]
    if fine:
        piece_spans = [
            [span(base + k, c, piece_w) for base in towers_from for k in range(CORES)]
            for c in range(PIECES)
        ]
        last_spans = [one for c in range(1, PIECES) for one in piece_spans[c]]
    else:
        last_spans = [span(base, 0, CORES * rows_w) for base in towers_from]

    def partly(rows, spans):
        lhs = [rows[:, one] for one in spans]
        rhs = [w_all[one, :] for one in spans]
        lhs = lhs[0] if len(lhs) == 1 else jnp.concatenate(lhs, axis=1)
        rhs = rhs[0] if len(rhs) == 1 else jnp.concatenate(rhs, axis=0)
        return jnp.dot(lhs, rhs, preferred_element_type=jnp.float32)

    def project(rows):
        return jnp.dot(rows, w_all[...], preferred_element_type=jnp.float32).astype(jnp.bfloat16)

    def mate_weights(c):
        for o in range(1, towers):
            view = shard_rows(lax.rem(mate + shards - CORES * o, shards), c)
            pltpu.make_async_copy(view, view, wc_recv.at[o - 1, c]).wait()

    def neighbours(act):
        for way in range(2):
            @pl.when(q_receives(way, 0))
            def _():
                act(q_all.at[z - 1 if way == 0 else z + 1], q_part.at[1 + way])

    def begin(rows, part):
        part[...] = partly(rows, first_spans)

    def extend(rows, part):
        part[...] += partly(rows, piece_spans[0])

    own_part = p_part.at[pl.ds(pl.multiple_of(x * rows_p, rows_p), rows_p)]
    for copy in locals_:
        copy.wait()
    other_w = w_all.at[pl.ds(pl.multiple_of(mate * rows_w, rows_w), rows_w)]
    pltpu.make_async_copy(other_w, other_w, own_recv).wait()
    begin(own_p, own_part)
    begin(q_all.at[z], q_part.at[0])
    pass_queries(0, 0)
    pass_weights(0)
    pass_queries(0, 1)
    neighbours(begin)
    mate_weights(0)
    if fine:
        extend(own_p, own_part)
        extend(q_all.at[z], q_part.at[0])
        neighbours(extend)
    for o in range(1, pairs):
        holder = lax.rem(x + pairs - o, pairs)
        view = p_rows(holder, 0)
        pltpu.make_async_copy(view, view, p_recv.at[o - 1, 0]).wait()
        p_part[p_piece(holder, 0), :] = partly(
            view, first_spans + piece_spans[0] if fine else first_spans
        )
    for step in range(1, n - 2):
        pass_queries(step, 0)
        if step == 1:
            pass_weights(1)
        pass_queries(step, 1)
    mate_weights(1)

    for o in range(pairs):
        holder = lax.rem(x + pairs - o, pairs)
        for h in range(PIECES):
            view = p_rows(holder, h)
            piece = p_piece(holder, h)
            if o and h:
                pltpu.make_async_copy(view, view, p_recv.at[o - 1, h]).wait()
                p_proj[piece, :] = project(view[...])
            else:
                whole = p_part[piece, :] + partly(view, last_spans)
                p_proj[piece, :] = whole.astype(jnp.bfloat16)

    for o in range(1, n):
        view = meta.at[lax.rem(z + n - o, n)]
        pltpu.make_async_copy(view, view, meta_recv.at[o - 1]).wait()

    tiles = pairs * rows_p // BLOCK
    first_tile = z * tiles
    row_index = lax.broadcasted_iota(jnp.int32, (BLOCK, BLOCK), 0)

    def stats_copy(block):
        return remote(
            stats_out.at[block], stats_in.at[z], st_send.at[block], st_recv.at[z], {"dp": block}
        )

    def meet(t, carry):
        away = lax.div(t + 1, 2)
        way = lax.rem(t + 1, 2)
        place = jnp.where(way == 0, z - away, z + away)
        block = jnp.clip(place, 0, n - 1)

        @pl.when((place >= 0) & (place < n))
        def _():
            @pl.when(away <= 1)
            def _():
                rest = partly(q_all.at[block], last_spans)
                q_proj[...] = (q_part[jnp.minimum(t, 2)] + rest).astype(jnp.bfloat16)

            @pl.when((away > 1) & (away < n - 1))
            def _():
                q_proj[...] = project(q_all[block])

            @pl.when(away == n - 1)
            def _():
                for h in range(PIECES):
                    part = pl.ds(h * piece_q, piece_q)
                    view = q_all.at[block, part]
                    pltpu.make_async_copy(view, view, q_recv.at[way, n - 2, h]).wait()
                    q_proj[part, :] = project(view[...])

            logits = lax.dot_general(
                p_proj[...], q_proj[...], (((1,), (1,)), ((), ())),
                preferred_element_type=jnp.float32,
            ) * scale
            info = meta[block]
            target = info[0:1, :]
            top = jnp.full((1, BLOCK), MASKED, jnp.float32)
            target_logit = jnp.zeros((1, BLOCK), jnp.float32)
            picks = []
            for k in range(tiles):
                tile = logits[k * BLOCK:(k + 1) * BLOCK, :]
                listed = info[1:2, :] == first_tile + k
                for l in range(1, max_list):
                    listed = listed | (info[l + 1:l + 2, :] == first_tile + k)
                is_target = row_index == target - (first_tile + k) * BLOCK
                chosen = listed | is_target
                picks.append((tile, chosen))
                top = jnp.maximum(
                    top, jnp.max(jnp.where(chosen, tile, MASKED), axis=0, keepdims=True)
                )
                target_logit += jnp.sum(jnp.where(is_target, tile, 0.0), axis=0, keepdims=True)
            total = jnp.zeros((1, BLOCK), jnp.float32)
            for tile, chosen in picks:
                total += jnp.sum(
                    jnp.where(chosen, jnp.exp(tile - top), 0.0), axis=0, keepdims=True
                )

            @pl.when(t == 0)
            def _():
                stats_in[z, 0:1, :] = top
                stats_in[z, 1:2, :] = total
                stats_in[z, 2:3, :] = target_logit

            @pl.when(t > 0)
            def _():
                stats_out[block, 0:1, :] = top
                stats_out[block, 1:2, :] = total
                stats_out[block, 2:3, :] = target_logit
                stats_copy(block).start()

        return carry

    lax.fori_loop(0, 2 * n - 1, meet, 0)

    for o in range(1, n):
        view = stats_in.at[lax.rem(z + o, n)]
        pltpu.make_async_copy(view, view, st_recv.at[lax.rem(z + o, n)]).wait()
    top = stats_in[0, 0:1, :]
    for i in range(1, n):
        top = jnp.maximum(top, stats_in[i, 0:1, :])
    total = jnp.zeros((1, BLOCK), jnp.float32)
    target_logit = jnp.zeros((1, BLOCK), jnp.float32)
    for i in range(n):
        total += stats_in[i, 1:2, :] * jnp.exp(stats_in[i, 0:1, :] - top)
        target_logit += stats_in[i, 2:3, :]
    out_ref[...] = top + jnp.log(total) - target_logit

    for copy in sent:
        copy.wait_send()
    for step in range(n - 1):
        for way in range(2):
            @pl.when(q_sends(way, step))
            def _():
                for h in range(PIECES):
                    q_copy(way, step, h).wait_send()
    for o in range(1, n):
        stats_copy(lax.rem(z + o, n)).wait_send()


def local(sizes, queries, passages, head_weight, positives, negative_ids, negative_count):
    n, shards, pairs, max_list = sizes
    towers = shards // CORES
    width = queries.shape[2]
    rows_p = passages.shape[1]
    meta_rows = -(-(max_list + 1) // 8) * 8
    hops = max(n - 1, 1)
    dma = pltpu.SemaphoreType.DMA
    far = max(towers - 1, 1)
    return pl.pallas_call(
        functools.partial(kernel, sizes),
        out_shape=jax.ShapeDtypeStruct((1, BLOCK), jnp.float32),
        in_specs=[
            pl.BlockSpec(memory_space=pltpu.HBM),
        ] * 6,
        out_specs=pl.BlockSpec(memory_space=pltpu.VMEM),
        scratch_shapes=[
            pltpu.VMEM((n, BLOCK, width), jnp.bfloat16),
            pltpu.VMEM((pairs * rows_p, width), jnp.bfloat16),
            pltpu.VMEM((pairs * rows_p, width), jnp.bfloat16),
            pltpu.VMEM((shards * head_weight.shape[0], width), jnp.bfloat16),
            pltpu.VMEM((n, meta_rows, BLOCK), jnp.int32),
            pltpu.VMEM((n, 8, BLOCK), jnp.float32),
            pltpu.VMEM((n, 8, BLOCK), jnp.float32),
            pltpu.SMEM(negative_ids.shape, jnp.int32),
            pltpu.SMEM(negative_count.shape, jnp.int32),
            pltpu.VMEM((pairs * rows_p, width), jnp.float32),
            pltpu.VMEM((3, BLOCK, width), jnp.float32),
            pltpu.VMEM((BLOCK, width), jnp.bfloat16),
            dma((6,)),
            dma((2, hops, PIECES)), dma((2, hops, PIECES)),
            dma((max(pairs - 1, 1), PIECES)), dma((max(pairs - 1, 1), PIECES)),
            dma, dma,
            dma((far, PIECES)), dma((far, PIECES)),
            dma((far, PIECES)), dma((far, PIECES)),
            dma((hops,)), dma((hops,)),
            dma((n,)), dma((n,)),
        ],
        compiler_params=pltpu.CompilerParams(
            collective_id=0, has_side_effects=True, vmem_limit_bytes=64 * 1024 * 1024
        ),
        name="retriever_loss",
    )(queries, passages, head_weight, positives, negative_ids, negative_count)


def solution(mesh):
    in_specs = (
        P("fsdp", ("dp", "query"), None),
        P("fsdp", ("dp", "query"), None),
        P("fsdp", None),
        P("fsdp", ("dp", "query")),
        P("fsdp", ("dp", "query"), None),
        P("fsdp", ("dp", "query")),
    )
    out_specs = P("fsdp", ("dp", "query"))

    def whole(queries, passages, head_weight, positives, negative_ids, negative_count):
        sizes = (
            mesh.shape["dp"], mesh.shape["fsdp"], mesh.shape["query"], negative_ids.shape[2]
        )
        return jax.shard_map(
            functools.partial(local, sizes),
            mesh=mesh, in_specs=in_specs, out_specs=out_specs, check_vma=False,
        )(queries, passages, head_weight, positives, negative_ids, negative_count)

    return whole
```

```python
import functools

import jax
import jax.numpy as jnp
from jax import lax
from jax.experimental import pallas as pl
from jax.experimental.pallas import tpu as pltpu
from jax.sharding import PartitionSpec as P

BLOCK = 128
CORES = 2
PIECES = 2
QUERY_PIECES = 4
MASKED = -1e30
MESH = pl.DeviceIdType.MESH


def kernel(
    sizes, q_ref, p_ref, w_ref, pos_ref, ids_ref, count_ref, out_ref,
    q_all, p_all, p_proj, w_all, meta, stats_out, stats_in, ids_own, count_own,
    p_part, q_part, q_proj,
    local_sem, q_send, q_recv, p_send, p_recv, own_send, own_recv,
    wy_send, wy_recv, wc_send, wc_recv, meta_send, meta_recv, st_send, st_recv,
):
    n, shards, pairs, max_list = sizes
    towers = shards // CORES
    rows_w = w_ref.shape[0]
    rows_p = p_ref.shape[1]
    width = q_ref.shape[2]
    piece_q = BLOCK // QUERY_PIECES
    piece_w = rows_w // PIECES
    piece_p = rows_p // PIECES
    scale = width ** -0.5
    z = lax.axis_index("dp")
    f = lax.axis_index("fsdp")
    x = lax.axis_index("query")
    core = lax.rem(f, CORES)
    mate = f + 1 - 2 * core

    def remote(src, dst, send, recv, where):
        return pltpu.make_async_remote_copy(
            src_ref=src, dst_ref=dst, send_sem=send, recv_sem=recv,
            device_id=where, device_id_type=MESH,
        )

    def shard_rows(shard, c):
        start = pl.multiple_of(shard * rows_w + c * piece_w, piece_w)
        return w_all.at[pl.ds(start, piece_w)]

    def p_rows(holder, h):
        return p_all.at[p_piece(holder, h)]

    def p_piece(holder, h):
        return pl.ds(pl.multiple_of(holder * rows_p + h * piece_p, piece_p), piece_p)

    own_w = w_all.at[pl.ds(pl.multiple_of(f * rows_w, rows_w), rows_w)]
    own_p = p_all.at[pl.ds(pl.multiple_of(x * rows_p, rows_p), rows_p)]
    lists_ = [
        pltpu.make_async_copy(pos_ref, meta.at[z, pl.ds(0, 1)], local_sem.at[3]),
        pltpu.make_async_copy(ids_ref, ids_own, local_sem.at[4]),
        pltpu.make_async_copy(count_ref, count_own, local_sem.at[5]),
    ]
    for copy in lists_:
        copy.start()
    locals_ = [
        pltpu.make_async_copy(w_ref, own_w, local_sem.at[0]),
        pltpu.make_async_copy(p_ref.at[0], own_p, local_sem.at[1]),
        pltpu.make_async_copy(q_ref.at[0], q_all.at[z], local_sem.at[2]),
    ]
    for copy in locals_:
        copy.start()

    barrier = pltpu.get_barrier_semaphore()
    friends = [{"dp": lax.rem(z + o, n)} for o in range(1, n)]
    friends += [{"query": lax.rem(x + o, pairs)} for o in range(1, pairs)]
    friends += [{"fsdp": lax.rem(f + CORES * o, shards)} for o in range(1, towers)]
    friends += [{"fsdp": mate}]
    for friend in friends:
        pl.semaphore_signal(barrier, inc=1, device_id=friend, device_id_type=MESH)

    for copy in lists_:
        copy.wait()
    live = count_own[0, 0]
    for l in range(max_list):
        entry = jnp.where(l < live, ids_own[0, 0, l], -1)
        meta[z, l + 1:l + 2, :] = jnp.full((1, BLOCK), entry, jnp.int32)
    pl.semaphore_wait(barrier, len(friends))

    def q_copy(way, step, h):
        block = z - step if way == 0 else z + step
        block = jnp.clip(block, 0, n - 1)
        view = q_all.at[block, pl.ds(h * piece_q, piece_q)]
        src = q_ref.at[0, pl.ds(h * piece_q, piece_q)] if step == 0 else view
        target = jnp.minimum(z + 1, n - 1) if way == 0 else jnp.maximum(z - 1, 0)
        return remote(src, view, q_send.at[way, step, h], q_recv.at[way, step, h], {"dp": target})

    def q_sends(way, step):
        if way == 0:
            return (z + 1 < n) & (z >= step)
        return (z >= 1) & (z + step < n)

    def q_wait(way, step, h):
        block = z - 1 - step if way == 0 else z + 1 + step
        block = jnp.clip(block, 0, n - 1)
        view = q_all.at[block, pl.ds(h * piece_q, piece_q)]
        pltpu.make_async_copy(view, view, q_recv.at[way, step, h]).wait()

    def q_receives(way, step):
        return z - 1 - step >= 0 if way == 0 else z + 1 + step < n

    for h in range(QUERY_PIECES):
        for way in range(2):
            @pl.when(q_sends(way, 0))
            def _():
                q_copy(way, 0, h).start()

    sent = []
    for c in range(PIECES):
        for o in range(1, towers):
            copy = remote(
                w_ref.at[pl.ds(c * piece_w, piece_w)], shard_rows(f, c),
                wy_send.at[o - 1, c], wy_recv.at[o - 1, c],
                {"fsdp": lax.rem(f + CORES * o, shards)},
            )
            copy.start()
            sent.append(copy)
    for h in range(PIECES):
        for o in range(1, pairs):
            copy = remote(
                p_ref.at[0, pl.ds(h * piece_p, piece_p)], p_rows(x, h),
                p_send.at[o - 1, h], p_recv.at[o - 1, h], {"query": lax.rem(x + o, pairs)},
            )
            copy.start()
            sent.append(copy)
    own_copy = remote(w_ref, own_w, own_send, own_recv, {"fsdp": mate})
    own_copy.start()
    sent.append(own_copy)
    for o in range(1, n):
        copy = remote(
            meta.at[z], meta.at[z], meta_send.at[o - 1], meta_recv.at[o - 1],
            {"dp": lax.rem(z + o, n)},
        )
        copy.start()
        sent.append(copy)

    def pass_queries(step, h):
        for way in range(2):
            @pl.when(q_receives(way, step))
            def _():
                q_wait(way, step, h)

            @pl.when(q_sends(way, step + 1))
            def _():
                q_copy(way, step + 1, h).start()

    def pass_weights(c):
        for o in range(1, towers):
            shard = lax.rem(f + shards - CORES * o, shards)
            view = shard_rows(shard, c)
            pltpu.make_async_copy(view, view, wy_recv.at[o - 1, c]).wait()
            copy = remote(view, view, wc_send.at[o - 1, c], wc_recv.at[o - 1, c], {"fsdp": mate})
            copy.start()
            sent.append(copy)

    def span(shard, c, depth):
        return pl.ds(pl.multiple_of(shard * rows_w + c * piece_w, depth), depth)

    fine = piece_w % 128 == 0
    towers_from = [lax.rem(f - core + CORES * o, shards) for o in range(1, towers)]
    first_spans = [span(f - core, 0, CORES * rows_w)]
    if fine:
        piece_spans = [
            [span(base + k, c, piece_w) for base in towers_from for k in range(CORES)]
            for c in range(PIECES)
        ]
        last_spans = [one for c in range(1, PIECES) for one in piece_spans[c]]
    else:
        last_spans = [span(base, 0, CORES * rows_w) for base in towers_from]

    def partly(rows, spans):
        lhs = [rows[:, one] for one in spans]
        rhs = [w_all[one, :] for one in spans]
        lhs = lhs[0] if len(lhs) == 1 else jnp.concatenate(lhs, axis=1)
        rhs = rhs[0] if len(rhs) == 1 else jnp.concatenate(rhs, axis=0)
        return jnp.dot(lhs, rhs, preferred_element_type=jnp.float32)

    def project(rows):
        return jnp.dot(rows, w_all[...], preferred_element_type=jnp.float32).astype(jnp.bfloat16)

    def mate_weights(c):
        for o in range(1, towers):
            view = shard_rows(lax.rem(mate + shards - CORES * o, shards), c)
            pltpu.make_async_copy(view, view, wc_recv.at[o - 1, c]).wait()

    def neighbours(act):
        for way in range(2):
            @pl.when(q_receives(way, 0))
            def _():
                act(q_all.at[z - 1 if way == 0 else z + 1], q_part.at[1 + way])

    def begin(rows, part):
        part[...] = partly(rows, first_spans)

    def extend(rows, part):
        part[...] += partly(rows, piece_spans[0])

    own_part = p_part.at[pl.ds(pl.multiple_of(x * rows_p, rows_p), rows_p)]
    for copy in locals_:
        copy.wait()
    other_w = w_all.at[pl.ds(pl.multiple_of(mate * rows_w, rows_w), rows_w)]
    pltpu.make_async_copy(other_w, other_w, own_recv).wait()
    begin(own_p, own_part)
    begin(q_all.at[z], q_part.at[0])
    for h in range(QUERY_PIECES):
        pass_queries(0, h)
    pass_weights(0)
    neighbours(begin)
    mate_weights(0)
    if fine:
        extend(own_p, own_part)
        extend(q_all.at[z], q_part.at[0])
        neighbours(extend)
    for o in range(1, pairs):
        holder = lax.rem(x + pairs - o, pairs)
        view = p_rows(holder, 0)
        pltpu.make_async_copy(view, view, p_recv.at[o - 1, 0]).wait()
        p_part[p_piece(holder, 0), :] = partly(
            view, first_spans + piece_spans[0] if fine else first_spans
        )
    for step in range(1, n - 2):
        for h in range(QUERY_PIECES):
            if step == 1 and h == QUERY_PIECES - 1:
                pass_weights(1)
            pass_queries(step, h)
    mate_weights(1)

    for o in range(pairs):
        holder = lax.rem(x + pairs - o, pairs)
        for h in range(PIECES):
            view = p_rows(holder, h)
            piece = p_piece(holder, h)
            if o and h:
                pltpu.make_async_copy(view, view, p_recv.at[o - 1, h]).wait()
                p_proj[piece, :] = project(view[...])
            else:
                whole = p_part[piece, :] + partly(view, last_spans)
                p_proj[piece, :] = whole.astype(jnp.bfloat16)

    for o in range(1, n):
        view = meta.at[lax.rem(z + n - o, n)]
        pltpu.make_async_copy(view, view, meta_recv.at[o - 1]).wait()

    tiles = pairs * rows_p // BLOCK
    first_tile = z * tiles
    row_index = lax.broadcasted_iota(jnp.int32, (BLOCK, BLOCK), 0)

    def stats_copy(block):
        return remote(
            stats_out.at[block], stats_in.at[z], st_send.at[block], st_recv.at[z], {"dp": block}
        )

    def meet(t, carry):
        away = lax.div(t + 1, 2)
        way = lax.rem(t + 1, 2)
        place = jnp.where(way == 0, z - away, z + away)
        block = jnp.clip(place, 0, n - 1)

        @pl.when((place >= 0) & (place < n))
        def _():
            @pl.when(away <= 1)
            def _():
                rest = partly(q_all.at[block], last_spans)
                q_proj[...] = (q_part[jnp.minimum(t, 2)] + rest).astype(jnp.bfloat16)

            @pl.when((away > 1) & (away < n - 1))
            def _():
                q_proj[...] = project(q_all[block])

            @pl.when(away == n - 1)
            def _():
                for h in range(QUERY_PIECES):
                    view = q_all.at[block, pl.ds(h * piece_q, piece_q)]
                    pltpu.make_async_copy(view, view, q_recv.at[way, n - 2, h]).wait()
                    if h % 2:
                        part = pl.ds((h - 1) * piece_q, 2 * piece_q)
                        q_proj[part, :] = project(q_all[block, part])

            logits = lax.dot_general(
                p_proj[...], q_proj[...], (((1,), (1,)), ((), ())),
                preferred_element_type=jnp.float32,
            ) * scale
            info = meta[block]
            target = info[0:1, :]
            top = jnp.full((1, BLOCK), MASKED, jnp.float32)
            target_logit = jnp.zeros((1, BLOCK), jnp.float32)
            picks = []
            for k in range(tiles):
                tile = logits[k * BLOCK:(k + 1) * BLOCK, :]
                listed = info[1:2, :] == first_tile + k
                for l in range(1, max_list):
                    listed = listed | (info[l + 1:l + 2, :] == first_tile + k)
                is_target = row_index == target - (first_tile + k) * BLOCK
                chosen = listed | is_target
                picks.append((tile, chosen))
                top = jnp.maximum(
                    top, jnp.max(jnp.where(chosen, tile, MASKED), axis=0, keepdims=True)
                )
                target_logit += jnp.sum(jnp.where(is_target, tile, 0.0), axis=0, keepdims=True)
            total = jnp.zeros((1, BLOCK), jnp.float32)
            for tile, chosen in picks:
                total += jnp.sum(
                    jnp.where(chosen, jnp.exp(tile - top), 0.0), axis=0, keepdims=True
                )

            @pl.when(t == 0)
            def _():
                stats_in[z, 0:1, :] = top
                stats_in[z, 1:2, :] = total
                stats_in[z, 2:3, :] = target_logit

            @pl.when(t > 0)
            def _():
                stats_out[block, 0:1, :] = top
                stats_out[block, 1:2, :] = total
                stats_out[block, 2:3, :] = target_logit
                stats_copy(block).start()

        return carry

    lax.fori_loop(0, 2 * n - 1, meet, 0)

    for o in range(1, n):
        view = stats_in.at[lax.rem(z + o, n)]
        pltpu.make_async_copy(view, view, st_recv.at[lax.rem(z + o, n)]).wait()
    top = stats_in[0, 0:1, :]
    for i in range(1, n):
        top = jnp.maximum(top, stats_in[i, 0:1, :])
    total = jnp.zeros((1, BLOCK), jnp.float32)
    target_logit = jnp.zeros((1, BLOCK), jnp.float32)
    for i in range(n):
        total += stats_in[i, 1:2, :] * jnp.exp(stats_in[i, 0:1, :] - top)
        target_logit += stats_in[i, 2:3, :]
    out_ref[...] = top + jnp.log(total) - target_logit

    for copy in sent:
        copy.wait_send()
    for step in range(n - 1):
        for way in range(2):
            @pl.when(q_sends(way, step))
            def _():
                for h in range(QUERY_PIECES):
                    q_copy(way, step, h).wait_send()
    for o in range(1, n):
        stats_copy(lax.rem(z + o, n)).wait_send()


def local(sizes, queries, passages, head_weight, positives, negative_ids, negative_count):
    n, shards, pairs, max_list = sizes
    towers = shards // CORES
    width = queries.shape[2]
    rows_p = passages.shape[1]
    meta_rows = -(-(max_list + 1) // 8) * 8
    hops = max(n - 1, 1)
    dma = pltpu.SemaphoreType.DMA
    far = max(towers - 1, 1)
    return pl.pallas_call(
        functools.partial(kernel, sizes),
        out_shape=jax.ShapeDtypeStruct((1, BLOCK), jnp.float32),
        in_specs=[
            pl.BlockSpec(memory_space=pltpu.HBM),
        ] * 6,
        out_specs=pl.BlockSpec(memory_space=pltpu.VMEM),
        scratch_shapes=[
            pltpu.VMEM((n, BLOCK, width), jnp.bfloat16),
            pltpu.VMEM((pairs * rows_p, width), jnp.bfloat16),
            pltpu.VMEM((pairs * rows_p, width), jnp.bfloat16),
            pltpu.VMEM((shards * head_weight.shape[0], width), jnp.bfloat16),
            pltpu.VMEM((n, meta_rows, BLOCK), jnp.int32),
            pltpu.VMEM((n, 8, BLOCK), jnp.float32),
            pltpu.VMEM((n, 8, BLOCK), jnp.float32),
            pltpu.SMEM(negative_ids.shape, jnp.int32),
            pltpu.SMEM(negative_count.shape, jnp.int32),
            pltpu.VMEM((pairs * rows_p, width), jnp.float32),
            pltpu.VMEM((3, BLOCK, width), jnp.float32),
            pltpu.VMEM((BLOCK, width), jnp.bfloat16),
            dma((6,)),
            dma((2, hops, QUERY_PIECES)), dma((2, hops, QUERY_PIECES)),
            dma((max(pairs - 1, 1), PIECES)), dma((max(pairs - 1, 1), PIECES)),
            dma, dma,
            dma((far, PIECES)), dma((far, PIECES)),
            dma((far, PIECES)), dma((far, PIECES)),
            dma((hops,)), dma((hops,)),
            dma((n,)), dma((n,)),
        ],
        compiler_params=pltpu.CompilerParams(
            collective_id=0, has_side_effects=True, vmem_limit_bytes=64 * 1024 * 1024
        ),
        name="retriever_loss",
    )(queries, passages, head_weight, positives, negative_ids, negative_count)


def solution(mesh):
    in_specs = (
        P("fsdp", ("dp", "query"), None),
        P("fsdp", ("dp", "query"), None),
        P("fsdp", None),
        P("fsdp", ("dp", "query")),
        P("fsdp", ("dp", "query"), None),
        P("fsdp", ("dp", "query")),
    )
    out_specs = P("fsdp", ("dp", "query"))

    def whole(queries, passages, head_weight, positives, negative_ids, negative_count):
        sizes = (
            mesh.shape["dp"], mesh.shape["fsdp"], mesh.shape["query"], negative_ids.shape[2]
        )
        return jax.shard_map(
            functools.partial(local, sizes),
            mesh=mesh, in_specs=in_specs, out_specs=out_specs, check_vma=False,
        )(queries, passages, head_weight, positives, negative_ids, negative_count)

    return whole
```

```python
import functools

import jax
import jax.numpy as jnp
from jax import lax
from jax.experimental import pallas as pl
from jax.experimental.pallas import tpu as pltpu
from jax.sharding import PartitionSpec as P

BLOCK = 128
CORES = 2
PIECES = 2
QUERY_PIECES = 4
MASKED = -1e30
MESH = pl.DeviceIdType.MESH


def kernel(
    sizes, q_ref, p_ref, w_ref, pos_ref, ids_ref, count_ref, out_ref,
    q_all, p_all, p_proj, w_all, meta, stats_out, stats_in, ids_own, count_own,
    p_part, q_part, q_proj,
    local_sem, q_send, q_recv, p_send, p_recv, own_send, own_recv,
    wy_send, wy_recv, wc_send, wc_recv, meta_send, meta_recv, st_send, st_recv,
):
    n, shards, pairs, max_list = sizes
    towers = shards // CORES
    rows_w = w_ref.shape[0]
    rows_p = p_ref.shape[1]
    width = q_ref.shape[2]
    piece_q = BLOCK // QUERY_PIECES
    piece_w = rows_w // PIECES
    piece_p = rows_p // PIECES
    scale = width ** -0.5
    z = lax.axis_index("dp")
    f = lax.axis_index("fsdp")
    x = lax.axis_index("query")
    core = lax.rem(f, CORES)
    mate = f + 1 - 2 * core

    def remote(src, dst, send, recv, where):
        return pltpu.make_async_remote_copy(
            src_ref=src, dst_ref=dst, send_sem=send, recv_sem=recv,
            device_id=where, device_id_type=MESH,
        )

    def shard_rows(shard, c):
        start = pl.multiple_of(shard * rows_w + c * piece_w, piece_w)
        return w_all.at[pl.ds(start, piece_w)]

    def p_rows(holder, h):
        return p_all.at[p_piece(holder, h)]

    def p_piece(holder, h):
        return pl.ds(pl.multiple_of(holder * rows_p + h * piece_p, piece_p), piece_p)

    own_w = w_all.at[pl.ds(pl.multiple_of(f * rows_w, rows_w), rows_w)]
    own_p = p_all.at[pl.ds(pl.multiple_of(x * rows_p, rows_p), rows_p)]
    lists_ = [
        pltpu.make_async_copy(pos_ref, meta.at[z, pl.ds(0, 1)], local_sem.at[3]),
        pltpu.make_async_copy(ids_ref, ids_own, local_sem.at[4]),
        pltpu.make_async_copy(count_ref, count_own, local_sem.at[5]),
    ]
    for copy in lists_:
        copy.start()
    locals_ = [
        pltpu.make_async_copy(w_ref, own_w, local_sem.at[0]),
        pltpu.make_async_copy(p_ref.at[0], own_p, local_sem.at[1]),
        pltpu.make_async_copy(q_ref.at[0], q_all.at[z], local_sem.at[2]),
    ]
    for copy in locals_:
        copy.start()

    barrier = pltpu.get_barrier_semaphore()
    friends = [{"dp": lax.rem(z + o, n)} for o in range(1, n)]
    friends += [{"query": lax.rem(x + o, pairs)} for o in range(1, pairs)]
    friends += [{"fsdp": lax.rem(f + CORES * o, shards)} for o in range(1, towers)]
    friends += [{"fsdp": mate}]
    for friend in friends:
        pl.semaphore_signal(barrier, inc=1, device_id=friend, device_id_type=MESH)

    for copy in lists_:
        copy.wait()
    live = count_own[0, 0]
    for l in range(max_list):
        entry = jnp.where(l < live, ids_own[0, 0, l], -1)
        meta[z, l + 1:l + 2, :] = jnp.full((1, BLOCK), entry, jnp.int32)
    pl.semaphore_wait(barrier, len(friends))

    def q_copy(way, step, h):
        block = z - step if way == 0 else z + step
        block = jnp.clip(block, 0, n - 1)
        view = q_all.at[block, pl.ds(h * piece_q, piece_q)]
        src = q_ref.at[0, pl.ds(h * piece_q, piece_q)] if step == 0 else view
        target = jnp.minimum(z + 1, n - 1) if way == 0 else jnp.maximum(z - 1, 0)
        return remote(src, view, q_send.at[way, step, h], q_recv.at[way, step, h], {"dp": target})

    def q_sends(way, step):
        if way == 0:
            return (z + 1 < n) & (z >= step)
        return (z >= 1) & (z + step < n)

    def q_wait(way, step, h):
        block = z - 1 - step if way == 0 else z + 1 + step
        block = jnp.clip(block, 0, n - 1)
        view = q_all.at[block, pl.ds(h * piece_q, piece_q)]
        pltpu.make_async_copy(view, view, q_recv.at[way, step, h]).wait()

    def q_receives(way, step):
        return z - 1 - step >= 0 if way == 0 else z + 1 + step < n

    for h in range(QUERY_PIECES):
        for way in range(2):
            @pl.when(q_sends(way, 0))
            def _():
                q_copy(way, 0, h).start()

    sent = []
    for c in range(PIECES):
        for o in range(1, towers):
            copy = remote(
                w_ref.at[pl.ds(c * piece_w, piece_w)], shard_rows(f, c),
                wy_send.at[o - 1, c], wy_recv.at[o - 1, c],
                {"fsdp": lax.rem(f + CORES * o, shards)},
            )
            copy.start()
            sent.append(copy)
    for h in range(PIECES):
        for o in range(1, pairs):
            copy = remote(
                p_ref.at[0, pl.ds(h * piece_p, piece_p)], p_rows(x, h),
                p_send.at[o - 1, h], p_recv.at[o - 1, h], {"query": lax.rem(x + o, pairs)},
            )
            copy.start()
            sent.append(copy)
    own_copy = remote(w_ref, own_w, own_send, own_recv, {"fsdp": mate})
    own_copy.start()
    sent.append(own_copy)
    for o in range(1, n):
        copy = remote(
            meta.at[z], meta.at[z], meta_send.at[o - 1], meta_recv.at[o - 1],
            {"dp": lax.rem(z + o, n)},
        )
        copy.start()
        sent.append(copy)

    def pass_queries(step, h):
        for near in range(2):
            for way in (1 - near, near):
                side = z < n // 2 if near == 0 else z >= n // 2

                @pl.when(side & q_receives(way, step))
                def _():
                    q_wait(way, step, h)

                @pl.when(side & q_sends(way, step + 1))
                def _():
                    q_copy(way, step + 1, h).start()

    def pass_weights(c):
        for o in range(1, towers):
            shard = lax.rem(f + shards - CORES * o, shards)
            view = shard_rows(shard, c)
            pltpu.make_async_copy(view, view, wy_recv.at[o - 1, c]).wait()
            copy = remote(view, view, wc_send.at[o - 1, c], wc_recv.at[o - 1, c], {"fsdp": mate})
            copy.start()
            sent.append(copy)

    def span(shard, c, depth):
        return pl.ds(pl.multiple_of(shard * rows_w + c * piece_w, depth), depth)

    fine = piece_w % 128 == 0
    towers_from = [lax.rem(f - core + CORES * o, shards) for o in range(1, towers)]
    first_spans = [span(f - core, 0, CORES * rows_w)]
    if fine:
        piece_spans = [
            [span(base + k, c, piece_w) for base in towers_from for k in range(CORES)]
            for c in range(PIECES)
        ]
        last_spans = [one for c in range(1, PIECES) for one in piece_spans[c]]
    else:
        last_spans = [span(base, 0, CORES * rows_w) for base in towers_from]

    def partly(rows, spans):
        lhs = [rows[:, one] for one in spans]
        rhs = [w_all[one, :] for one in spans]
        lhs = lhs[0] if len(lhs) == 1 else jnp.concatenate(lhs, axis=1)
        rhs = rhs[0] if len(rhs) == 1 else jnp.concatenate(rhs, axis=0)
        return jnp.dot(lhs, rhs, preferred_element_type=jnp.float32)

    def project(rows):
        return jnp.dot(rows, w_all[...], preferred_element_type=jnp.float32).astype(jnp.bfloat16)

    def mate_weights(c):
        for o in range(1, towers):
            view = shard_rows(lax.rem(mate + shards - CORES * o, shards), c)
            pltpu.make_async_copy(view, view, wc_recv.at[o - 1, c]).wait()

    def neighbours(act):
        for way in range(2):
            @pl.when(q_receives(way, 0))
            def _():
                act(q_all.at[z - 1 if way == 0 else z + 1], q_part.at[1 + way])

    def begin(rows, part):
        part[...] = partly(rows, first_spans)

    def extend(rows, part):
        part[...] += partly(rows, piece_spans[0])

    own_part = p_part.at[pl.ds(pl.multiple_of(x * rows_p, rows_p), rows_p)]
    for copy in locals_:
        copy.wait()
    other_w = w_all.at[pl.ds(pl.multiple_of(mate * rows_w, rows_w), rows_w)]
    pltpu.make_async_copy(other_w, other_w, own_recv).wait()
    begin(own_p, own_part)
    begin(q_all.at[z], q_part.at[0])
    for h in range(QUERY_PIECES):
        pass_queries(0, h)
    pass_weights(0)
    neighbours(begin)
    mate_weights(0)
    if fine:
        extend(own_p, own_part)
        extend(q_all.at[z], q_part.at[0])
        neighbours(extend)
    for o in range(1, pairs):
        holder = lax.rem(x + pairs - o, pairs)
        view = p_rows(holder, 0)
        pltpu.make_async_copy(view, view, p_recv.at[o - 1, 0]).wait()
        p_part[p_piece(holder, 0), :] = partly(
            view, first_spans + piece_spans[0] if fine else first_spans
        )
    for step in range(1, n - 2):
        for h in range(QUERY_PIECES):
            if step == 1 and h == QUERY_PIECES - 1:
                pass_weights(1)
            pass_queries(step, h)
    mate_weights(1)

    for o in range(pairs):
        holder = lax.rem(x + pairs - o, pairs)
        for h in range(PIECES):
            view = p_rows(holder, h)
            piece = p_piece(holder, h)
            if o and h:
                pltpu.make_async_copy(view, view, p_recv.at[o - 1, h]).wait()
                p_proj[piece, :] = project(view[...])
            else:
                whole = p_part[piece, :] + partly(view, last_spans)
                p_proj[piece, :] = whole.astype(jnp.bfloat16)

    for o in range(1, n):
        view = meta.at[lax.rem(z + n - o, n)]
        pltpu.make_async_copy(view, view, meta_recv.at[o - 1]).wait()

    tiles = pairs * rows_p // BLOCK
    first_tile = z * tiles
    row_index = lax.broadcasted_iota(jnp.int32, (BLOCK, BLOCK), 0)

    def stats_copy(block):
        return remote(
            stats_out.at[block], stats_in.at[z], st_send.at[block], st_recv.at[z], {"dp": block}
        )

    def meet(t, carry):
        away = lax.div(t + 1, 2)
        way = lax.rem(t + 1, 2)
        place = jnp.where(way == 0, z - away, z + away)
        block = jnp.clip(place, 0, n - 1)

        @pl.when((place >= 0) & (place < n))
        def _():
            @pl.when(away <= 1)
            def _():
                rest = partly(q_all.at[block], last_spans)
                q_proj[...] = (q_part[jnp.minimum(t, 2)] + rest).astype(jnp.bfloat16)

            @pl.when((away > 1) & (away < n - 1))
            def _():
                q_proj[...] = project(q_all[block])

            @pl.when(away == n - 1)
            def _():
                for h in range(QUERY_PIECES):
                    view = q_all.at[block, pl.ds(h * piece_q, piece_q)]
                    pltpu.make_async_copy(view, view, q_recv.at[way, n - 2, h]).wait()
                    if h % 2:
                        part = pl.ds((h - 1) * piece_q, 2 * piece_q)
                        q_proj[part, :] = project(q_all[block, part])

            logits = lax.dot_general(
                p_proj[...], q_proj[...], (((1,), (1,)), ((), ())),
                preferred_element_type=jnp.float32,
            ) * scale
            info = meta[block]
            target = info[0:1, :]
            top = jnp.full((1, BLOCK), MASKED, jnp.float32)
            target_logit = jnp.zeros((1, BLOCK), jnp.float32)
            picks = []
            for k in range(tiles):
                tile = logits[k * BLOCK:(k + 1) * BLOCK, :]
                listed = info[1:2, :] == first_tile + k
                for l in range(1, max_list):
                    listed = listed | (info[l + 1:l + 2, :] == first_tile + k)
                is_target = row_index == target - (first_tile + k) * BLOCK
                chosen = listed | is_target
                picks.append((tile, chosen))
                top = jnp.maximum(
                    top, jnp.max(jnp.where(chosen, tile, MASKED), axis=0, keepdims=True)
                )
                target_logit += jnp.sum(jnp.where(is_target, tile, 0.0), axis=0, keepdims=True)
            total = jnp.zeros((1, BLOCK), jnp.float32)
            for tile, chosen in picks:
                total += jnp.sum(
                    jnp.where(chosen, jnp.exp(tile - top), 0.0), axis=0, keepdims=True
                )

            @pl.when(t == 0)
            def _():
                stats_in[z, 0:1, :] = top
                stats_in[z, 1:2, :] = total
                stats_in[z, 2:3, :] = target_logit

            @pl.when(t > 0)
            def _():
                stats_out[block, 0:1, :] = top
                stats_out[block, 1:2, :] = total
                stats_out[block, 2:3, :] = target_logit
                stats_copy(block).start()

        return carry

    lax.fori_loop(0, 2 * n - 1, meet, 0)

    for o in range(1, n):
        view = stats_in.at[lax.rem(z + o, n)]
        pltpu.make_async_copy(view, view, st_recv.at[lax.rem(z + o, n)]).wait()
    top = stats_in[0, 0:1, :]
    for i in range(1, n):
        top = jnp.maximum(top, stats_in[i, 0:1, :])
    total = jnp.zeros((1, BLOCK), jnp.float32)
    target_logit = jnp.zeros((1, BLOCK), jnp.float32)
    for i in range(n):
        total += stats_in[i, 1:2, :] * jnp.exp(stats_in[i, 0:1, :] - top)
        target_logit += stats_in[i, 2:3, :]
    out_ref[...] = top + jnp.log(total) - target_logit

    for copy in sent:
        copy.wait_send()
    for step in range(n - 1):
        for way in range(2):
            @pl.when(q_sends(way, step))
            def _():
                for h in range(QUERY_PIECES):
                    q_copy(way, step, h).wait_send()
    for o in range(1, n):
        stats_copy(lax.rem(z + o, n)).wait_send()


def local(sizes, queries, passages, head_weight, positives, negative_ids, negative_count):
    n, shards, pairs, max_list = sizes
    towers = shards // CORES
    width = queries.shape[2]
    rows_p = passages.shape[1]
    meta_rows = -(-(max_list + 1) // 8) * 8
    hops = max(n - 1, 1)
    dma = pltpu.SemaphoreType.DMA
    far = max(towers - 1, 1)
    return pl.pallas_call(
        functools.partial(kernel, sizes),
        out_shape=jax.ShapeDtypeStruct((1, BLOCK), jnp.float32),
        in_specs=[
            pl.BlockSpec(memory_space=pltpu.HBM),
        ] * 6,
        out_specs=pl.BlockSpec(memory_space=pltpu.VMEM),
        scratch_shapes=[
            pltpu.VMEM((n, BLOCK, width), jnp.bfloat16),
            pltpu.VMEM((pairs * rows_p, width), jnp.bfloat16),
            pltpu.VMEM((pairs * rows_p, width), jnp.bfloat16),
            pltpu.VMEM((shards * head_weight.shape[0], width), jnp.bfloat16),
            pltpu.VMEM((n, meta_rows, BLOCK), jnp.int32),
            pltpu.VMEM((n, 8, BLOCK), jnp.float32),
            pltpu.VMEM((n, 8, BLOCK), jnp.float32),
            pltpu.SMEM(negative_ids.shape, jnp.int32),
            pltpu.SMEM(negative_count.shape, jnp.int32),
            pltpu.VMEM((pairs * rows_p, width), jnp.float32),
            pltpu.VMEM((3, BLOCK, width), jnp.float32),
            pltpu.VMEM((BLOCK, width), jnp.bfloat16),
            dma((6,)),
            dma((2, hops, QUERY_PIECES)), dma((2, hops, QUERY_PIECES)),
            dma((max(pairs - 1, 1), PIECES)), dma((max(pairs - 1, 1), PIECES)),
            dma, dma,
            dma((far, PIECES)), dma((far, PIECES)),
            dma((far, PIECES)), dma((far, PIECES)),
            dma((hops,)), dma((hops,)),
            dma((n,)), dma((n,)),
        ],
        compiler_params=pltpu.CompilerParams(
            collective_id=0, has_side_effects=True, vmem_limit_bytes=64 * 1024 * 1024
        ),
        name="retriever_loss",
    )(queries, passages, head_weight, positives, negative_ids, negative_count)


def solution(mesh):
    in_specs = (
        P("fsdp", ("dp", "query"), None),
        P("fsdp", ("dp", "query"), None),
        P("fsdp", None),
        P("fsdp", ("dp", "query")),
        P("fsdp", ("dp", "query"), None),
        P("fsdp", ("dp", "query")),
    )
    out_specs = P("fsdp", ("dp", "query"))

    def whole(queries, passages, head_weight, positives, negative_ids, negative_count):
        sizes = (
            mesh.shape["dp"], mesh.shape["fsdp"], mesh.shape["query"], negative_ids.shape[2]
        )
        return jax.shard_map(
            functools.partial(local, sizes),
            mesh=mesh, in_specs=in_specs, out_specs=out_specs, check_vma=False,
        )(queries, passages, head_weight, positives, negative_ids, negative_count)

    return whole
```
